128 devices in a mesh: loop: 16 (over z, y), head: 8 (over x, core).
Axes of the slice: x: 4, y: 4, z: 4, core: 2. Of those that a mesh axis runs over, the one named last changes fastest.
Arguments:
- features: bfloat16 [49152, 768], P(('loop', 'head')), may hold values from -6 to 6
- node_order: int32 [49152], P('loop'), may hold values from 0 to 3071, as said below
- tile_cols: int32 [384, 29], replicated, may hold values from -1 to 383, as said below
- norm_gain: float32 [768], replicated
- w_query: bfloat16 [768, 768], replicated
- w_key: bfloat16 [768, 768], replicated
- w_value: bfloat16 [768, 768], replicated, may hold values from -0.21875 to 0.21875
- w_out: bfloat16 [768, 768], replicated, may hold values from -0.21875 to 0.21875
Outputs:
- mixed: bfloat16 [49152, 768], P(('loop', 'head'))
The draws below stay inside these ranges and needn't reach their ends.
Inputs may be any that keep to these rules, and one draw needn't show every extreme that they name: `node_order`: each run of 3072 entries, in order, is a permutation of 0 to 3071. `tile_cols`: row r names distinct clusters: r itself in slot 0, then 20 other clusters of its own slab (slab s holds clusters s * 24 to (s + 1) * 24 - 1), then clusters of other slabs or -1. The rows of one slab name between 1 and 12 different clusters of each other slab, exactly 12 for some pairs of slabs; some row uses all 29 slots.
All inputs are finite; a program needn't handle non-finite values.
Results may differ from the reference program's by a relative error of at most 0.0065.
The reference program's roundings to bfloat16 on the way (of `normed`, `weights` and `attended`) count: a program that leaves them out, or rounds other values in their place, can miss the bound.
Values may be sent and summed in bfloat16 or wider, within the bound.
A program may use at most 128 MiB of HBM per device.

```python
import math
import jax
import jax.numpy as jnp
from jax import lax

D = 768
HEADS = 8
HDIM = 96
BLOCK = 128
C_DEV = 24
CAP = 12
LOC = 20
TMAX = 29
SLAB = 3072
CLUSTERS = 384
NODES = 49152


def common_part(key):
    return jax.random.normal(key, (D, D), jnp.float32)


def draw_w_query(key, part):
    shared = common_part(key)
    key = jax.random.fold_in(key, 11)
    own = jax.random.normal(key, (D, D), jnp.float32)
    return ((0.6 * shared + own) * (1.0 / math.sqrt(1.36 * D))).astype(jnp.bfloat16)


def draw_w_key(key, part):
    shared = common_part(key)
    key = jax.random.fold_in(key, 13)
    own = jax.random.normal(key, (D, D), jnp.float32)
    return ((0.6 * shared + own) * (1.0 / math.sqrt(1.36 * D))).astype(jnp.bfloat16)


def draw_norm_gain(key, part):
    key = jax.random.fold_in(key, 5)
    lowest, highest = (0.6, 1.6)
    spread = jax.random.uniform(key, (D,), jnp.float32)
    return jnp.exp(math.log(lowest) + spread * (math.log(highest) - math.log(lowest)))


def draw_node_order(key, part):
    key = jax.random.fold_in(key, 3)
    number = NODES // SLAB
    orders = jax.vmap(lambda subkey: jax.random.permutation(subkey, SLAB))(jax.random.split(key, number))
    return orders.reshape(NODES).astype(jnp.int32)


def draw_tile_cols(key, part):
    key = jax.random.fold_in(key, 7)
    slabs = CLUSTERS // C_DEV
    far_slots = TMAX - 1 - LOC
    near_key, count_key, pick_key, order_key, full_key = jax.random.split(key, 5)
    offsets = jax.vmap(lambda subkey: jax.random.permutation(subkey, C_DEV - 1)[:LOC])(jax.random.split(near_key, CLUSTERS)) + 1
    cluster_ids = jnp.arange(CLUSTERS, dtype=jnp.int32)
    starts = cluster_ids // C_DEV * C_DEV
    near_cols = starts[:, None] + (cluster_ids[:, None] % C_DEV + offsets) % C_DEV
    counts = jax.random.randint(count_key, (slabs, slabs), 1, CAP + 1)
    full_slab = jax.random.randint(full_key, (), 0, slabs)
    target = jnp.arange(slabs)[:, None]
    anchor = jnp.arange(slabs)[None, :]
    counts = jnp.where((anchor == (target + 1) % slabs) | (target == full_slab), CAP, counts)
    counts = jnp.where(target == anchor, 0, counts)
    picks = jax.vmap(lambda subkey: jax.random.permutation(subkey, C_DEV))(jax.random.split(pick_key, slabs * slabs))
    picks = picks.reshape(slabs, slabs, C_DEV)[:, :, :CAP]
    chosen = anchor[:, :, None] * C_DEV + picks
    usable = jnp.arange(CAP)[None, None, :] < counts[:, :, None]
    chosen = jnp.where(usable, chosen, -1).reshape(slabs, slabs * CAP)
    usable = usable.reshape(slabs, slabs * CAP)
    noise = jax.vmap(lambda subkey: jax.random.permutation(subkey, slabs * CAP))(jax.random.split(order_key, slabs))
    ranking = jnp.where(usable, 0, slabs * CAP) + noise
    ordering = jnp.argsort(ranking, axis=1, stable=True)
    chosen = jnp.take_along_axis(chosen, ordering, axis=1)
    span = far_slots * C_DEV
    filler = jnp.full((slabs, max(span - slabs * CAP, 0)), -1, jnp.int32)
    padded = jnp.concatenate([chosen.astype(jnp.int32), filler], axis=1)[:, :span]
    far_cols = padded.reshape(slabs, far_slots, C_DEV).transpose(0, 2, 1).reshape(CLUSTERS, far_slots)
    return jnp.concatenate([cluster_ids[:, None], near_cols.astype(jnp.int32), far_cols], axis=1).astype(jnp.int32)


def levels(key, dims, pieces, least, high):
    level, own = 1.0, jax.random.fold_in(key, 6)
    for dim, blocks in pieces:
        steps = jnp.exp(jax.random.uniform(jax.random.fold_in(own, dim), (blocks,), jnp.float32, least / len(pieces), high / len(pieces)))
        level = level * jnp.repeat(steps, dims[dim] // blocks).reshape([-1 if axis == dim else 1 for axis in range(len(dims))])
    return level


def scatter_about(rng, dims, scale, limit, cuts=(), kind=jnp.bfloat16):
    values = scale * jax.random.normal(rng, dims, jnp.float32)
    if cuts:
        values = values * levels(rng, dims, cuts, -0.22, 0.18)
    return jnp.clip(values, -limit, limit).astype(kind)


def setup_inputs(seed: int = 0) -> dict:
    arg_keys = jax.random.split(jax.random.key(seed), 9)
    return {
        "features": scatter_about(arg_keys[0], (NODES, D), 1.0, 6.0, ((0, 128),)),
        "node_order": draw_node_order(jax.random.fold_in(arg_keys[8], 71), 0),
        "tile_cols": draw_tile_cols(jax.random.fold_in(arg_keys[8], 71), 0),
        "norm_gain": draw_norm_gain(jax.random.fold_in(arg_keys[8], 71), 0),
        "w_query": draw_w_query(jax.random.fold_in(arg_keys[8], 71), 0),
        "w_key": draw_w_key(jax.random.fold_in(arg_keys[8], 71), 0),
        "w_value": scatter_about(arg_keys[6], (D, D), D ** -0.5, 0.21875),
        "w_out": scatter_about(arg_keys[7], (D, D), D ** -0.5, 0.21875),
    }


def reference(features, node_order, tile_cols, norm_gain, w_query, w_key, w_value, w_out):
    widened = features.astype(jnp.float32)
    meansq = lax.optimization_barrier(jnp.mean(widened * widened, axis=-1, keepdims=True))
    normed = (widened * lax.rsqrt(meansq + 1e-06) * norm_gain).astype(jnp.bfloat16)
    query = jnp.dot(normed, w_query, preferred_element_type=jnp.float32).astype(jnp.bfloat16)
    keys = jnp.dot(normed, w_key, preferred_element_type=jnp.float32).astype(jnp.bfloat16)
    values = jnp.dot(normed, w_value, preferred_element_type=jnp.float32).astype(jnp.bfloat16)
    shifts = jnp.arange(NODES, dtype=jnp.int32) // SLAB * SLAB
    source = node_order.astype(jnp.int32) + shifts
    query = query[source].reshape(CLUSTERS, BLOCK, HEADS, HDIM)
    keys = keys[source].reshape(CLUSTERS, BLOCK, HEADS, HDIM)
    values = values[source].reshape(CLUSTERS, BLOCK, HEADS, HDIM)
    usable = tile_cols >= 0
    columns = jnp.where(usable, tile_cols, 0).astype(jnp.int32)
    scale = 1.0 / math.sqrt(HDIM)

    def attend(packed):
        block_query, block_cols, block_ok = packed
        near_keys = keys[block_cols].astype(jnp.float32)
        near_values = values[block_cols].astype(jnp.float32)
        scores = jnp.einsum('qhe,tkhe->hqtk', block_query.astype(jnp.float32), near_keys) * scale
        allowed = block_ok[None, None, :, None]
        scores = jnp.where(allowed, scores, -1e+30)
        highest = lax.optimization_barrier(jnp.max(scores, axis=(2, 3), keepdims=True))
        expo = jnp.where(allowed, jnp.exp(scores - highest), 0.0)
        weights = (expo / lax.optimization_barrier(jnp.sum(expo, axis=(2, 3), keepdims=True))).astype(jnp.bfloat16)
        result = jnp.einsum('hqtk,tkhe->qhe', weights.astype(jnp.float32), near_values)
        return result.astype(jnp.bfloat16)
    attended = lax.map(attend, (query, columns, usable)).reshape(NODES, D)
    return jnp.dot(attended, w_out, preferred_element_type=jnp.float32).astype(jnp.bfloat16)
```

```python
import functools
import math

import jax
import jax.numpy as jnp
from jax import lax
from jax.experimental import pallas as pl
from jax.experimental.pallas import tpu as pltpu
from jax.sharding import PartitionSpec as P

HEADS = 8
HDIM = 96
D = 768
BLOCK = 128
CL = 24
LOC = 21
FAR = 8
ROWS = 384
SLAB = 3072
RING = 4
SCALE2 = math.log2(math.e) / math.sqrt(HDIM)
MESH = pl.DeviceIdType.MESH
VMEM = pl.BlockSpec(memory_space=pltpu.VMEM)
SMEM = pl.BlockSpec(memory_space=pltpu.SMEM)
LIMIT = 56 * 1024 * 1024
NEG = -1e30
F32 = jnp.float32
BF16 = jnp.bfloat16


def nt(a, b):
    return lax.dot_general(a, b, (((1,), (1,)), ((), ())), preferred_element_type=F32)


def nn(a, b):
    return jnp.dot(a, b, preferred_element_type=F32)


def greet(partners):
    barrier = pltpu.get_barrier_semaphore()
    for partner in partners:
        pl.semaphore_signal(barrier, inc=1, device_id=partner, device_id_type=MESH)
    pl.semaphore_wait(barrier, len(partners))


def share_kernel(feat_ref, gain_ref, out_ref, send, recv):
    line = lax.axis_index("loop")
    head = lax.axis_index("head")
    x, core = head // 2, head % 2
    xr, xl, xo = (x + 1) % RING, (x + 3) % RING, (x + 2) % RING
    other = (line, x * 2 + 1 - core)
    right = (line, xr * 2 + core)
    left = (line, xl * 2 + core)
    greet([other, right, left])
    wide = feat_ref[...].astype(F32)
    meansq = jnp.mean(wide * wide, axis=-1, keepdims=True)
    out_ref[head] = (wide * lax.rsqrt(meansq + 1e-06) * gain_ref[...]).astype(BF16)
    half = ROWS // 2
    lo, hi, full = (0, half), (half, half), (0, ROWS)
    b_r, b_l, b_o = xr * 2 + core, xl * 2 + core, xo * 2 + core
    plan = [
        (head, full, other),
        (head, hi, right),
        (head, lo, right),
        (head, lo, left),
        (head, hi, left),
        (b_l, hi, right),
        (b_r, lo, left),
        (b_l, hi, other),
        (b_l, lo, other),
        (b_r, lo, other),
        (b_r, hi, other),
        (b_o, hi, other),
        (b_o, lo, other),
    ]

    def copy(k):
        block, (start, size), device = plan[k]
        ref = out_ref.at[block, pl.ds(start, size)]
        return pltpu.make_async_remote_copy(
            src_ref=ref,
            dst_ref=ref,
            send_sem=send.at[k],
            recv_sem=recv.at[k],
            device_id=device,
            device_id_type=MESH,
        )

    for k in (1, 3, 2, 4, 0):
        copy(k).start()
    copy(1).wait_recv()
    copy(5).start()
    copy(7).start()
    copy(3).wait_recv()
    copy(6).start()
    copy(9).start()
    copy(2).wait_recv()
    copy(8).start()
    copy(4).wait_recv()
    copy(10).start()
    copy(5).wait_recv()
    copy(11).start()
    copy(6).wait_recv()
    copy(12).start()
    for k in (0, 7, 8, 9, 10, 11, 12):
        copy(k).wait_recv()
    for k in range(13):
        copy(k).wait_send()


def share(features, gain):
    return pl.pallas_call(
        share_kernel,
        out_shape=jax.ShapeDtypeStruct((HEADS, ROWS, D), BF16),
        in_specs=[VMEM, VMEM],
        out_specs=VMEM,
        scratch_shapes=[pltpu.SemaphoreType.DMA((13,)), pltpu.SemaphoreType.DMA((13,))],
        compiler_params=pltpu.CompilerParams(
            collective_id=0, has_side_effects=True, vmem_limit_bytes=LIMIT
        ),
    )(features, gain)


def project_kernel(x_ref, order_ref, wq_ref, wk_ref, wv_ref, kv_ref, q_ref, w_scr, t_scr):
    head = lax.axis_index("head")
    pick_row = lax.broadcasted_iota(jnp.int32, (HDIM, D), 0) + head * HDIM
    pick_col = lax.broadcasted_iota(jnp.int32, (HDIM, D), 1)
    pick = jnp.where(pick_row == pick_col, 1.0, 0.0).astype(BF16)
    for i, w_ref in enumerate((wk_ref, wv_ref, wq_ref)):
        w_scr[i * HDIM : (i + 1) * HDIM, :] = nt(pick, w_ref[...]).astype(BF16)
    for b in range(HEADS):
        t_scr[:, b * ROWS : (b + 1) * ROWS] = nt(w_scr[...], x_ref[b]).astype(BF16)
    width = 512
    for chunk in range(SLAB // width):
        order = order_ref[:, chunk * width : (chunk + 1) * width]
        every = lax.broadcasted_iota(jnp.int32, (SLAB, width), 0)
        picker = jnp.where(every == order, 1.0, 0.0).astype(BF16)
        moved = nn(t_scr[...], picker).astype(BF16)
        for i in range(width // BLOCK):
            part = moved[:, i * BLOCK : (i + 1) * BLOCK]
            kv_ref[chunk * (width // BLOCK) + i] = part[: 2 * HDIM]
            q_ref[chunk * (width // BLOCK) + i] = part[2 * HDIM :]


def project(x, order, wq, wk, wv):
    return pl.pallas_call(
        project_kernel,
        out_shape=(
            jax.ShapeDtypeStruct((CL, 2 * HDIM, BLOCK), BF16),
            jax.ShapeDtypeStruct((CL, HDIM, BLOCK), BF16),
        ),
        in_specs=[VMEM] * 5,
        out_specs=(VMEM, VMEM),
        scratch_shapes=[pltpu.VMEM((3 * HDIM, D), BF16), pltpu.VMEM((3 * HDIM, SLAB), BF16)],
        compiler_params=pltpu.CompilerParams(vmem_limit_bytes=LIMIT),
    )(x, order, wq, wk, wv)


def place():
    line = lax.axis_index("loop")
    head = lax.axis_index("head")
    z, y, core = line // RING, line % RING, head % 2
    return line, head, z, y, core


def on_kv_ring(step):
    line, head, z, y, core = place()
    return ((z + step * (1 - core)) % RING * RING + (y + step * core) % RING, head)


def on_q_ring(step):
    line, head, z, y, core = place()
    return ((z + step * core) % RING * RING + (y + step * (1 - core)) % RING, head)


def ring_copies(own_ref, table_ref, pos, device, send, recv):
    half = CL // 2
    before, after = (pos + RING - 1) % RING, (pos + 1) % RING
    plan = [
        (None, half, 1),
        (None, 0, 1),
        (None, 0, RING - 1),
        (None, half, RING - 1),
        (before, half, 1),
        (after, 0, RING - 1),
    ]

    def copy(k):
        block, start, step = plan[k]
        if block is None:
            src, block = own_ref.at[pl.ds(start, half)], pos
        else:
            src = table_ref.at[block, pl.ds(start, half)]
        return pltpu.make_async_remote_copy(
            src_ref=src,
            dst_ref=table_ref.at[block, pl.ds(start, half)],
            send_sem=send.at[k],
            recv_sem=recv.at[k],
            device_id=device(step),
            device_id_type=MESH,
        )

    return copy


def pack(total, top):
    lane = lax.broadcasted_iota(jnp.int32, total.shape, 1)
    return jnp.where(lane >= 112, top, total)


def attend_near(c, row, cols_ref, kv_ref, q_ref, near_ref, s_scr):
    query = jnp.transpose(q_ref[c].astype(F32)).astype(BF16)
    ones = jnp.ones((BLOCK - HDIM, 2 * BLOCK), BF16)
    first = cols_ref[row, 0] // CL * CL
    cols = [cols_ref[row, t] - first for t in range(LOC)]
    top = None
    for t in range(0, LOC - 1, 2):
        keys = jnp.concatenate([kv_ref[cols[t], :HDIM], kv_ref[cols[t + 1], :HDIM]], axis=1)
        score = nn(query, keys)
        s_scr[t // 2] = score
        top = score if top is None else jnp.maximum(top, score)
    last = nn(query, kv_ref[cols[LOC - 1], :HDIM])
    top = jnp.maximum(jnp.maximum(top[:, :BLOCK], top[:, BLOCK:]), last)
    top = jnp.max(top, axis=1, keepdims=True)
    expo = jnp.exp2((last - top) * SCALE2).astype(BF16)
    values = jnp.concatenate([kv_ref[cols[LOC - 1], HDIM:], ones[:, :BLOCK]], axis=0)
    total = nt(expo, values)
    for t in range(0, LOC - 1, 2):
        expo = jnp.exp2((s_scr[t // 2] - top) * SCALE2).astype(BF16)
        values = jnp.concatenate([kv_ref[cols[t], HDIM:], kv_ref[cols[t + 1], HDIM:]], axis=1)
        total += nt(expo, jnp.concatenate([values, ones], axis=0))
    near_ref[c] = pack(total, top)


def near_kernel(
    cols_ref, kv_ref, q_ref, kvt_ref, qt_ref, near_ref, s_scr, kv_send, kv_recv, q_send, q_recv
):
    line, head, z, y, core = place()
    greet([on_kv_ring(1), on_kv_ring(3), on_q_ring(1), on_q_ring(3)])
    kv_pos = z * (1 - core) + y * core
    q_pos = z * core + y * (1 - core)
    kv_copy = ring_copies(kv_ref, kvt_ref, kv_pos, on_kv_ring, kv_send, kv_recv)
    q_copy = ring_copies(q_ref, qt_ref, q_pos, on_q_ring, q_send, q_recv)
    for k in (0, 2):
        kv_copy(k).start()
    for k in (0, 2):
        q_copy(k).start()
    for k in (1, 3):
        kv_copy(k).start()
    for k in (1, 3):
        q_copy(k).start()
    kvt_ref[kv_pos] = kv_ref[...]
    qt_ref[q_pos] = q_ref[...]

    def some(first, last):
        def step(c, carry):
            attend_near(c, line * CL + c, cols_ref, kv_ref, q_ref, near_ref, s_scr)
            return carry

        lax.fori_loop(first, last, step, 0)

    some(0, 14)
    for copy in (kv_copy, q_copy):
        copy(0).wait_recv()
        copy(4).start()
        copy(2).wait_recv()
        copy(5).start()
    some(14, CL)
    for copy in (kv_copy, q_copy):
        for k in (1, 3, 4, 5):
            copy(k).wait_recv()
        for k in range(6):
            copy(k).wait_send()


def near(cols, kv, q):
    return pl.pallas_call(
        near_kernel,
        out_shape=(
            jax.ShapeDtypeStruct((RING, CL, 2 * HDIM, BLOCK), BF16),
            jax.ShapeDtypeStruct((RING, CL, HDIM, BLOCK), BF16),
            jax.ShapeDtypeStruct((CL, BLOCK, BLOCK), F32),
        ),
        in_specs=[SMEM, VMEM, VMEM],
        out_specs=(VMEM, VMEM, VMEM),
        scratch_shapes=[
            pltpu.VMEM((LOC // 2, BLOCK, 2 * BLOCK), F32),
            pltpu.SemaphoreType.DMA((6,)),
            pltpu.SemaphoreType.DMA((6,)),
            pltpu.SemaphoreType.DMA((6,)),
            pltpu.SemaphoreType.DMA((6,)),
        ],
        compiler_params=pltpu.CompilerParams(
            collective_id=1, has_side_effects=True, vmem_limit_bytes=LIMIT
        ),
    )(cols, kv, q)


UNROLL = 4
QROWS = RING * CL
ITEMS = QROWS * FAR


def far_kernel(pos_ref, kvt_ref, qt_ref, part_ref, acc, tile_list, row_list):
    lane = lax.broadcasted_iota(jnp.int32, (BLOCK, BLOCK), 1)
    empty = jnp.where(lane >= 112, NEG, 0.0)

    def scan(r, count):
        acc[r] = empty
        for slot in range(FAR):
            tile = pos_ref[r, slot]
            tile_list[count] = tile
            row_list[count] = r
            count = count + jnp.where(tile >= 0, 1, 0)
        tile_list[count] = -1
        return count + (count & 1)

    count = lax.fori_loop(0, QROWS, scan, 0)
    for i in range(2 * UNROLL):
        tile_list[count + i] = -1
        row_list[count + i] = QROWS
    acc[QROWS] = empty
    rounds = (count + 2 * UNROLL - 1) // (2 * UNROLL)
    ones = jnp.ones((BLOCK - HDIM, 2 * BLOCK), BF16)

    def item(step, carry):
        found = []
        for u in range(UNROLL):
            at = (step * UNROLL + u) * 2
            row = row_list[at]
            tile_a, tile_b = tile_list[at], tile_list[at + 1]
            bias_a = jnp.where(tile_a >= 0, 0.0, NEG)
            bias_b = jnp.where(tile_b >= 0, 0.0, NEG)
            a, b = jnp.maximum(tile_a, 0), jnp.maximum(tile_b, 0)
            query = jnp.transpose(qt_ref[jnp.minimum(row, QROWS - 1)].astype(F32)).astype(BF16)
            keys = jnp.concatenate([kvt_ref[a, :HDIM], kvt_ref[b, :HDIM]], axis=1)
            score = nn(query, keys)
            score = jnp.concatenate([score[:, :BLOCK] + bias_a, score[:, BLOCK:] + bias_b], axis=1)
            top = jnp.max(score, axis=1, keepdims=True)
            expo = jnp.exp2((score - top) * SCALE2).astype(BF16)
            values = jnp.concatenate([kvt_ref[a, HDIM:], kvt_ref[b, HDIM:]], axis=1)
            total = nt(expo, jnp.concatenate([values, ones], axis=0))
            found.append((row, top, total))
        for row, top, total in found:
            old = acc[row]
            old_top = old[:, 127:128]
            new_top = jnp.maximum(old_top, top)
            total = old * jnp.exp2((old_top - new_top) * SCALE2) + total * jnp.exp2(
                (top - new_top) * SCALE2
            )
            acc[row] = pack(total, new_top)
        return carry

    lax.fori_loop(0, rounds, item, 0)

    def finish(r, carry):
        value, lse = settle(acc[r])
        high = lse.astype(BF16).astype(F32)
        rest = lse - high
        middle = rest.astype(BF16).astype(F32)
        low = rest - middle
        value = jnp.where(lane == HDIM, high, value)
        value = jnp.where(lane == HDIM + 1, middle, value)
        value = jnp.where(lane == HDIM + 2, low, value)
        part_ref[r] = value.astype(BF16)
        return carry

    lax.fori_loop(0, QROWS, finish, 0)


def settle(packed):
    total = packed[:, HDIM : HDIM + 1]
    top = packed[:, 127:128]
    filled = total > 0.0
    safe = jnp.where(filled, total, 1.0)
    lse = jnp.where(filled, top * SCALE2 + jnp.log2(safe), NEG)
    return packed * (1.0 / safe), lse


def far(pos, kvt, qt):
    return pl.pallas_call(
        far_kernel,
        out_shape=jax.ShapeDtypeStruct((QROWS, BLOCK, BLOCK), BF16),
        in_specs=[SMEM, VMEM, VMEM],
        out_specs=VMEM,
        scratch_shapes=[
            pltpu.VMEM((QROWS + 1, BLOCK, BLOCK), F32),
            pltpu.SMEM((ITEMS + 4 * UNROLL,), jnp.int32),
            pltpu.SMEM((ITEMS + 4 * UNROLL,), jnp.int32),
        ],
        compiler_params=pltpu.CompilerParams(vmem_limit_bytes=LIMIT),
    )(pos, kvt, qt)


def join_kernel(near_ref, part_ref, out_ref, back, stage, b_send, b_recv, o_send, o_recv):
    line, head, z, y, core = place()
    peers = [(line, (head + d) % HEADS) for d in range(1, HEADS)]
    ring = [on_q_ring(d) for d in (1, 2, 3)]
    greet(ring + peers)
    pos = z * core + y * (1 - core)

    def back_copy(d):
        return pltpu.make_async_remote_copy(
            src_ref=part_ref.at[(pos + d) % RING],
            dst_ref=back.at[d],
            send_sem=b_send.at[d],
            recv_sem=b_recv.at[d],
            device_id=ring[d - 1],
            device_id_type=MESH,
        )

    for d in (2, 1, 3):
        back_copy(d).start()
    for d in (1, 3, 2):
        back_copy(d).wait_recv()

    def joined(j):
        blocks = []
        for i in range(3):
            c = j * 3 + i
            value, lse = settle(near_ref[c])
            values, lses = [value], [lse]
            for d in range(RING):
                packed = (part_ref[pos, c] if d == 0 else back[d, c]).astype(F32)
                values.append(packed)
                lses.append(
                    packed[:, HDIM : HDIM + 1]
                    + packed[:, HDIM + 1 : HDIM + 2]
                    + packed[:, HDIM + 2 : HDIM + 3]
                )
            top = functools.reduce(jnp.maximum, lses)
            scales = [jnp.exp2(one - top) for one in lses]
            whole = functools.reduce(jnp.add, scales)
            total = sum(v * s for v, s in zip(values, scales)) * (1.0 / whole)
            blocks.append(jnp.transpose(total)[:HDIM].astype(BF16))
        return jnp.concatenate(blocks, axis=1)

    def out_copy(d):
        return pltpu.make_async_remote_copy(
            src_ref=stage.at[d],
            dst_ref=out_ref.at[head],
            send_sem=o_send.at[d],
            recv_sem=o_recv.at[d],
            device_id=(line, (head + d) % HEADS),
            device_id_type=MESH,
        )

    def step(d, carry):
        stage[d] = joined((head + d) % HEADS)
        out_copy(d).start()
        return carry

    lax.fori_loop(1, HEADS, step, 0)
    out_ref[head] = joined(head)
    for d in range(1, HEADS):
        out_copy(d).wait_recv()
    for d in range(1, HEADS):
        out_copy(d).wait_send()
    for d in (1, 2, 3):
        back_copy(d).wait_send()


def join(near_part, part):
    return pl.pallas_call(
        join_kernel,
        out_shape=jax.ShapeDtypeStruct((HEADS, HDIM, ROWS), BF16),
        in_specs=[VMEM, VMEM],
        out_specs=VMEM,
        scratch_shapes=[
            pltpu.VMEM((RING, CL, BLOCK, BLOCK), BF16),
            pltpu.VMEM((HEADS, HDIM, ROWS), BF16),
            pltpu.SemaphoreType.DMA((RING,)),
            pltpu.SemaphoreType.DMA((RING,)),
            pltpu.SemaphoreType.DMA((HEADS,)),
            pltpu.SemaphoreType.DMA((HEADS,)),
        ],
        compiler_params=pltpu.CompilerParams(
            collective_id=2, has_side_effects=True, vmem_limit_bytes=LIMIT
        ),
    )(near_part, part)


def far_positions(tile_cols):
    line, head, z, y, core = place()
    grid = tile_cols[:, LOC:].reshape(RING, RING, CL, FAR)
    along_y = lax.dynamic_index_in_dim(grid, z, 0, keepdims=False)
    along_z = lax.dynamic_index_in_dim(grid, y, 1, keepdims=False)
    cols = jnp.where(core == 0, along_y, along_z).reshape(QROWS, FAR)
    slab, within = cols // CL, cols % CL
    slab_z, slab_y = slab // RING, slab % RING
    mine = jnp.where(core == 0, slab_y == y, slab_z == z) & (cols >= 0)
    index = jnp.where(core == 0, slab_z, slab_y)
    return jnp.where(mine, index * CL + within, -1)


def body(features, node_order, tile_cols, norm_gain, w_query, w_key, w_value, w_out):
    x = share(features, norm_gain.reshape(1, D))
    kv, q = project(x, node_order.reshape(1, SLAB), w_query, w_key, w_value)
    kvt, qt, near_part = near(tile_cols, kv, q)
    part = far(
        far_positions(tile_cols),
        kvt.reshape(QROWS, 2 * HDIM, BLOCK),
        qt.reshape(QROWS, HDIM, BLOCK),
    )
    merged = join(near_part, part.reshape(RING, CL, BLOCK, BLOCK))
    merged = merged.reshape(D, ROWS)
    return lax.dot_general(
        merged, w_out, (((0,), (0,)), ((), ())), preferred_element_type=F32
    ).astype(BF16)


def solution(mesh):
    in_specs = (P(("loop", "head"), None), P("loop"), P(), P(), P(), P(), P(), P())
    out_specs = P(("loop", "head"), None)
    return jax.shard_map(body, mesh=mesh, in_specs=in_specs, out_specs=out_specs, check_vma=False)
```

```python
import functools
import math

import jax
import jax.numpy as jnp
from jax import lax
from jax.experimental import pallas as pl
from jax.experimental.pallas import tpu as pltpu
from jax.sharding import PartitionSpec as P

HEADS = 8
HDIM = 96
D = 768
BLOCK = 128
CL = 24
LOC = 21
FAR = 8
ROWS = 384
SLAB = 3072
RING = 4
SCALE2 = math.log2(math.e) / math.sqrt(HDIM)
MESH = pl.DeviceIdType.MESH
VMEM = pl.BlockSpec(memory_space=pltpu.VMEM)
SMEM = pl.BlockSpec(memory_space=pltpu.SMEM)
LIMIT = 44 * 1024 * 1024
NEG = -1e30
F32 = jnp.float32
BF16 = jnp.bfloat16


def nt(a, b):
    return lax.dot_general(a, b, (((1,), (1,)), ((), ())), preferred_element_type=F32)


def nn(a, b):
    return jnp.dot(a, b, preferred_element_type=F32)


def greet(partners):
    barrier = pltpu.get_barrier_semaphore()
    for partner in partners:
        pl.semaphore_signal(barrier, inc=1, device_id=partner, device_id_type=MESH)


def meet(partners):
    pl.semaphore_wait(pltpu.get_barrier_semaphore(), len(partners))


def pinned(x):
    return pltpu.with_memory_space_constraint(x, pltpu.VMEM)


def place():
    line = lax.axis_index("loop")
    head = lax.axis_index("head")
    z, y, core = line // RING, line % RING, head % 2
    return line, head, z, y, core


def on_kv_ring(step):
    line, head, z, y, core = place()
    return ((z + step * (1 - core)) % RING * RING + (y + step * core) % RING, head)


def on_q_ring(step):
    line, head, z, y, core = place()
    return ((z + step * core) % RING * RING + (y + step * (1 - core)) % RING, head)


def share_copies(x_ref, send, recv):
    line, head, z, y, core = place()
    x = head // 2
    xr, xl, xo = (x + 1) % RING, (x + 3) % RING, (x + 2) % RING
    other = (line, x * 2 + 1 - core)
    right = (line, xr * 2 + core)
    left = (line, xl * 2 + core)
    half = ROWS // 2
    lo, hi, full = (0, half), (half, half), (0, ROWS)
    b_r, b_l, b_o = xr * 2 + core, xl * 2 + core, xo * 2 + core
    plan = [
        (head, full, other),
        (head, hi, right),
        (head, lo, right),
        (head, lo, left),
        (head, hi, left),
        (b_l, hi, right),
        (b_r, lo, left),
        (b_l, hi, other),
        (b_l, lo, other),
        (b_r, lo, other),
        (b_r, hi, other),
        (b_o, hi, other),
        (b_o, lo, other),
    ]

    def copy(k):
        block, (start, size), device = plan[k]
        ref = x_ref.at[block, pl.ds(start, size)]
        return pltpu.make_async_remote_copy(
            src_ref=ref,
            dst_ref=ref,
            send_sem=send.at[k],
            recv_sem=recv.at[k],
            device_id=device,
            device_id_type=MESH,
        )

    blocks = [xr * 2 + core, xl * 2 + core, xo * 2 + core]
    others = [xr * 2 + 1 - core, xl * 2 + 1 - core, xo * 2 + 1 - core]
    return copy, [other, right, left], x * 2 + 1 - core, blocks, others


def ring_copies(own_ref, table_ref, pos, device, send, recv):
    half = CL // 2
    before, after = (pos + RING - 1) % RING, (pos + 1) % RING
    plan = [
        (None, half, 1),
        (None, 0, 1),
        (None, 0, RING - 1),
        (None, half, RING - 1),
        (before, half, 1),
        (after, 0, RING - 1),
    ]

    def copy(k):
        block, start, step = plan[k]
        if block is None:
            src, block = own_ref.at[pl.ds(start, half)], pos
        else:
            src = table_ref.at[block, pl.ds(start, half)]
        return pltpu.make_async_remote_copy(
            src_ref=src,
            dst_ref=table_ref.at[block, pl.ds(start, half)],
            send_sem=send.at[k],
            recv_sem=recv.at[k],
            device_id=device(step),
            device_id_type=MESH,
        )

    return copy


def pack(total, top):
    lane = lax.broadcasted_iota(jnp.int32, total.shape, 1)
    return jnp.where(lane >= 112, top, total)


GROUP = 4
PAIRS = LOC // 2


def attend_near(first, cols_ref, kv_ref, q_ref, near_ref, s_scr):
    ones = jnp.ones((BLOCK - HDIM, 2 * BLOCK), BF16)
    group = range(GROUP)
    query = [jnp.transpose(q_ref[first + u].astype(F32)).astype(BF16) for u in group]
    cols = [[cols_ref[first + u, t] for t in range(LOC)] for u in group]
    tops = [None] * GROUP
    for p in range(PAIRS):
        for u in group:
            a, b = cols[u][2 * p], cols[u][2 * p + 1]
            score = nn(query[u], jnp.concatenate([kv_ref[a, :HDIM], kv_ref[b, :HDIM]], axis=1))
            s_scr[u, p] = score
            tops[u] = score if p == 0 else jnp.maximum(tops[u], score)
    last = [nn(query[u], kv_ref[cols[u][LOC - 1], :HDIM]) for u in group]
    total = []
    for u in group:
        top = jnp.maximum(jnp.maximum(tops[u][:, :BLOCK], tops[u][:, BLOCK:]), last[u])
        tops[u] = jnp.max(top, axis=1, keepdims=True)
    for u in group:
        expo = jnp.exp2((last[u] - tops[u]) * SCALE2).astype(BF16)
        values = jnp.concatenate([kv_ref[cols[u][LOC - 1], HDIM:], ones[:, :BLOCK]], axis=0)
        total.append(nt(expo, values))
    for p in range(PAIRS):
        for u in group:
            a, b = cols[u][2 * p], cols[u][2 * p + 1]
            expo = jnp.exp2((s_scr[u, p] - tops[u]) * SCALE2).astype(BF16)
            values = jnp.concatenate([kv_ref[a, HDIM:], kv_ref[b, HDIM:]], axis=1)
            total[u] += nt(expo, jnp.concatenate([values, ones], axis=0))
    for u in group:
        near_ref[first + u] = pack(total[u], tops[u])


CHUNK = 512
CHUNKS = SLAB // CHUNK


def near_kernel(
    feat_ref,
    gain_ref,
    order_ref,
    cols_ref,
    wq_ref,
    wk_ref,
    wv_ref,
    kvt_ref,
    qt_ref,
    near_ref,
    x_scr,
    w_scr,
    t_scr,
    pick_scr,
    kv_scr,
    q_scr,
    s_scr,
    x_send,
    x_recv,
    kv_send,
    kv_recv,
    q_send,
    q_recv,
):
    line, head, z, y, core = place()
    copy, partners, next_block, blocks, others = share_copies(x_scr, x_send, x_recv)
    partners = partners + [on_kv_ring(1), on_kv_ring(3), on_q_ring(1), on_q_ring(3)]
    greet(partners)
    wide = feat_ref[...].astype(F32)
    meansq = jnp.mean(wide * wide, axis=-1, keepdims=True)
    x_scr[head] = (wide * lax.rsqrt(meansq + 1e-06) * gain_ref[...]).astype(BF16)
    meet(partners)
    for k in (1, 3, 2, 4, 0):
        copy(k).start()

    def picker(c, carry):
        every = lax.broadcasted_iota(jnp.int32, (SLAB, CHUNK), 0)
        order = order_ref[:, pl.ds(pl.multiple_of(c * CHUNK, CHUNK), CHUNK)]
        pick_scr[c] = jnp.where(every == order, 1.0, 0.0).astype(BF16)
        return carry

    def project(b):
        columns = pl.ds(pl.multiple_of(b * ROWS, BLOCK), ROWS)
        t_scr[:, columns] = nt(w_scr[...], x_scr[b]).astype(BF16)

    pick_row = lax.broadcasted_iota(jnp.int32, (HDIM, D), 0) + head * HDIM
    pick_col = lax.broadcasted_iota(jnp.int32, (HDIM, D), 1)
    pick = jnp.where(pick_row == pick_col, 1.0, 0.0).astype(BF16)
    for i, w_ref in enumerate((wk_ref, wv_ref, wq_ref)):
        w_scr[i * HDIM : (i + 1) * HDIM, :] = nt(pick, w_ref[...]).astype(BF16)
    project(head)
    lax.fori_loop(0, CHUNKS // 2, picker, 0)
    copy(0).wait_recv()
    project(next_block)
    copy(1).wait_recv()
    copy(5).start()
    copy(7).start()
    copy(3).wait_recv()
    copy(6).start()
    copy(9).start()
    lax.fori_loop(CHUNKS // 2, CHUNKS, picker, 0)
    copy(2).wait_recv()
    copy(8).start()
    project(blocks[1])
    copy(4).wait_recv()
    copy(10).start()
    project(blocks[0])
    copy(7).wait_recv()
    copy(8).wait_recv()
    project(others[1])
    copy(9).wait_recv()
    copy(10).wait_recv()
    project(others[0])
    copy(5).wait_recv()
    copy(11).start()
    copy(6).wait_recv()
    copy(12).start()
    project(blocks[2])
    copy(11).wait_recv()
    copy(12).wait_recv()
    project(others[2])

    def move(c, carry):
        moved = nn(t_scr[...], pick_scr[c]).astype(BF16)
        for i in range(CHUNK // BLOCK):
            part = moved[:, i * BLOCK : (i + 1) * BLOCK]
            kv_scr[c * (CHUNK // BLOCK) + i] = part[: 2 * HDIM]
            q_scr[c * (CHUNK // BLOCK) + i] = part[2 * HDIM :]
        return carry

    kv_pos = z * (1 - core) + y * core
    q_pos = z * core + y * (1 - core)
    kv_copy = ring_copies(kv_scr, kvt_ref, kv_pos, on_kv_ring, kv_send, kv_recv)
    q_copy = ring_copies(q_scr, qt_ref, q_pos, on_q_ring, q_send, q_recv)
    lax.fori_loop(0, CHUNKS // 2, move, 0)
    for one in (kv_copy, q_copy):
        one(2).start()
        one(1).start()
    lax.fori_loop(CHUNKS // 2, CHUNKS, move, 0)
    for one in (kv_copy, q_copy):
        one(0).start()
        one(3).start()
    kvt_ref[kv_pos] = kv_scr[...]
    qt_ref[q_pos] = q_scr[...]

    def some(first, last):
        def step(g, carry):
            attend_near(g * GROUP, cols_ref, kv_scr, q_scr, near_ref, s_scr)
            return carry

        lax.fori_loop(first, last, step, 0)

    some(0, 4)
    for one in (kv_copy, q_copy):
        one(2).wait_recv()
        one(5).start()
    some(4, CL // GROUP)
    for one in (kv_copy, q_copy):
        one(0).wait_recv()
        one(4).start()
    for one in (kv_copy, q_copy):
        for k in (1, 3, 4, 5):
            one(k).wait_recv()
        for k in range(6):
            one(k).wait_send()
    for k in range(13):
        copy(k).wait_send()


def near(features, gain, order, cols, wq, wk, wv):
    return pl.pallas_call(
        near_kernel,
        out_shape=(
            pltpu.VMEM((RING, CL, 2 * HDIM, BLOCK), BF16),
            pltpu.VMEM((RING, CL, HDIM, BLOCK), BF16),
            pltpu.VMEM((CL, BLOCK, BLOCK), F32),
        ),
        in_specs=[VMEM, VMEM, VMEM, SMEM, VMEM, VMEM, VMEM],
        out_specs=(VMEM, VMEM, VMEM),
        scratch_shapes=[
            pltpu.VMEM((HEADS, ROWS, D), BF16),
            pltpu.VMEM((3 * HDIM, D), BF16),
            pltpu.VMEM((3 * HDIM, SLAB), BF16),
            pltpu.VMEM((CHUNKS, SLAB, CHUNK), BF16),
            pltpu.VMEM((CL, 2 * HDIM, BLOCK), BF16),
            pltpu.VMEM((CL, HDIM, BLOCK), BF16),
            pltpu.VMEM((GROUP, PAIRS, BLOCK, 2 * BLOCK), F32),
            pltpu.SemaphoreType.DMA((13,)),
            pltpu.SemaphoreType.DMA((13,)),
            pltpu.SemaphoreType.DMA((6,)),
            pltpu.SemaphoreType.DMA((6,)),
            pltpu.SemaphoreType.DMA((6,)),
            pltpu.SemaphoreType.DMA((6,)),
        ],
        compiler_params=pltpu.CompilerParams(
            collective_id=1, has_side_effects=True, vmem_limit_bytes=LIMIT
        ),
    )(features, gain, order, cols, wq, wk, wv)


UNROLL = 8
QROWS = RING * CL
ITEMS = QROWS * FAR
SUM_LOW, TOP_HIGH, TOP_MID, TOP_LOW = 104, 112, 118, 123


def far_kernel(pos_ref, kvt_ref, qt_ref, part_ref, acc, top_acc, tile_list, row_list):
    lane = lax.broadcasted_iota(jnp.int32, (BLOCK, BLOCK), 1)
    lowest = jnp.full((BLOCK, BLOCK), NEG, F32)
    nothing = jnp.zeros((BLOCK, BLOCK), F32)

    def scan(r, count):
        acc[r] = nothing
        top_acc[r] = lowest
        for slot in range(FAR):
            tile = pos_ref[r, slot]
            tile_list[count] = tile
            row_list[count] = r
            count = count + jnp.where(tile >= 0, 1, 0)
        tile_list[count] = -1
        return count + (count & 1)

    count = lax.fori_loop(0, QROWS, scan, 0)
    for i in range(2 * UNROLL):
        tile_list[count + i] = -1
        row_list[count + i] = QROWS
    acc[QROWS] = nothing
    top_acc[QROWS] = lowest
    rounds = (count + 2 * UNROLL - 1) // (2 * UNROLL)
    ones = jnp.ones((BLOCK - HDIM, 2 * BLOCK), BF16)

    def item(step, carry):
        rows, pairs, scores = [], [], []
        for u in range(UNROLL):
            at = (step * UNROLL + u) * 2
            row = row_list[at]
            tile_a, tile_b = tile_list[at], tile_list[at + 1]
            a, b = jnp.maximum(tile_a, 0), jnp.maximum(tile_b, 0)
            query = jnp.transpose(qt_ref[jnp.minimum(row, QROWS - 1)].astype(F32)).astype(BF16)
            score = nn(query, jnp.concatenate([kvt_ref[a, :HDIM], kvt_ref[b, :HDIM]], axis=1))
            score_a = score[:, :BLOCK] + jnp.where(tile_a >= 0, 0.0, NEG)
            score_b = score[:, BLOCK:] + jnp.where(tile_b >= 0, 0.0, NEG)
            rows.append(row)
            pairs.append((a, b))
            scores.append(jnp.concatenate([score_a, score_b], axis=1))
        tops = [
            jnp.max(jnp.maximum(s[:, :BLOCK], s[:, BLOCK:]), axis=1, keepdims=True) for s in scores
        ]
        expos = [jnp.exp2((s - t) * SCALE2).astype(BF16) for s, t in zip(scores, tops)]
        totals = []
        for expo, (a, b) in zip(expos, pairs):
            values = jnp.concatenate([kvt_ref[a, HDIM:], kvt_ref[b, HDIM:]], axis=1)
            totals.append(nt(expo, jnp.concatenate([values, ones], axis=0)))
        for row, top, total in zip(rows, tops, totals):
            top = jnp.broadcast_to(top, (BLOCK, BLOCK))
            old_top = top_acc[row]
            new_top = jnp.maximum(old_top, top)
            acc[row] = acc[row] * jnp.exp2((old_top - new_top) * SCALE2) + total * jnp.exp2(
                (top - new_top) * SCALE2
            )
            top_acc[row] = new_top
        return carry

    lax.fori_loop(0, rounds, item, 0)
    is_mid = ((lane >= SUM_LOW) & (lane < TOP_HIGH)) | ((lane >= TOP_MID) & (lane < TOP_LOW))
    is_low = lane >= TOP_LOW

    def finish(step, carry):
        for u in range(2):
            r = step * 2 + u
            value = jnp.where(lane >= TOP_HIGH, top_acc[r], acc[r])
            high = value.astype(BF16).astype(F32)
            rest = value - high
            mid = rest.astype(BF16).astype(F32)
            out = jnp.where(is_mid, mid, jnp.where(is_low, rest - mid, high))
            part_ref[r] = out.astype(BF16)
        return carry

    lax.fori_loop(0, QROWS // 2, finish, 0)


def far(pos, kvt, qt):
    return pl.pallas_call(
        far_kernel,
        out_shape=pltpu.VMEM((QROWS, BLOCK, BLOCK), BF16),
        in_specs=[SMEM, VMEM, VMEM],
        out_specs=VMEM,
        scratch_shapes=[
            pltpu.VMEM((QROWS + 1, BLOCK, BLOCK), F32),
            pltpu.VMEM((QROWS + 1, BLOCK, BLOCK), F32),
            pltpu.SMEM((ITEMS + 4 * UNROLL,), jnp.int32),
            pltpu.SMEM((ITEMS + 4 * UNROLL,), jnp.int32),
        ],
        compiler_params=pltpu.CompilerParams(vmem_limit_bytes=24 * 1024 * 1024),
    )(pos, pinned(kvt), pinned(qt))


PIECE = 6


def join_kernel(near_ref, part_ref, out_ref, back, relay, stage, b_send, b_recv, o_send, o_recv):
    line, head, z, y, core = place()
    x = head // 2
    partners = [on_q_ring(1), on_q_ring(3)]
    partners += [(line, (head + d) % HEADS) for d in range(1, HEADS)]
    greet(partners)
    meet(partners)
    pos = z * core + y * (1 - core)
    order = (2, 1, 3, 0)

    def rows(k):
        return pl.ds((x + order[k]) % RING * PIECE, PIECE)

    def copy(src, dst, k, step):
        return pltpu.make_async_remote_copy(
            src_ref=src,
            dst_ref=dst,
            send_sem=b_send.at[k],
            recv_sem=b_recv.at[k],
            device_id=on_q_ring(step),
            device_id_type=MESH,
        )

    def direct(step, k):
        way = 0 if step == 1 else 1
        src = part_ref.at[(pos + step) % RING, rows(k)]
        return copy(src, back.at[way, rows(k)], 4 * way + k, step)

    def first_leg(k):
        step = 1 if k % 2 == 0 else 3
        return copy(part_ref.at[(pos + 2) % RING, rows(k)], relay.at[k], 8 + k, step)

    def second_leg(k):
        step = 1 if k % 2 == 0 else 3
        return copy(relay.at[k], back.at[2, rows(k)], 12 + k, step)

    for k in range(2):
        first_leg(k).start()
    for k in range(2):
        direct(1, k).start()
        direct(3, k).start()
        first_leg(k + 2).start()
    for k in range(2, 4):
        direct(1, k).start()
        direct(3, k).start()

    spread_row = lax.broadcasted_iota(jnp.int32, (BLOCK, 2 * BLOCK), 0)
    spread_col = lax.broadcasted_iota(jnp.int32, (BLOCK, 2 * BLOCK), 1)
    is_top = (spread_row == TOP_HIGH) | (spread_row == TOP_MID) | (spread_row == TOP_LOW)
    is_sum = (spread_row == HDIM) | (spread_row == SUM_LOW)
    spread = jnp.where(
        spread_col < BLOCK, jnp.where(is_top, 1.0, 0.0), jnp.where(is_sum, 1.0, 0.0)
    ).astype(BF16)

    def joined(j):
        blocks = []
        for i in range(3):
            c = j * 3 + i
            mine = near_ref[c]
            packed = [part_ref[pos, c], back[0, c], back[1, c], back[2, c]]
            both = nn(jnp.concatenate(packed, axis=0), spread)
            values = [mine] + [one.astype(F32) for one in packed]
            tops = [jnp.broadcast_to(mine[:, 127:128], (BLOCK, BLOCK))]
            sums = [jnp.broadcast_to(mine[:, HDIM : HDIM + 1], (BLOCK, BLOCK))]
            for g in range(RING):
                tops.append(both[g * BLOCK : (g + 1) * BLOCK, :BLOCK])
                sums.append(both[g * BLOCK : (g + 1) * BLOCK, BLOCK:])
            top = functools.reduce(jnp.maximum, tops)
            scales = [jnp.exp2((one - top) * SCALE2) for one in tops]
            whole = sum(a * b for a, b in zip(sums, scales))
            total = sum(a * b for a, b in zip(values, scales)) / whole
            blocks.append(jnp.transpose(total)[:HDIM].astype(BF16))
        return jnp.concatenate(blocks, axis=1)

    def out_copy(j, sender):
        return pltpu.make_async_remote_copy(
            src_ref=stage.at[j],
            dst_ref=out_ref.at[sender],
            send_sem=o_send.at[j],
            recv_sem=o_recv.at[sender],
            device_id=(line, j),
            device_id_type=MESH,
        )

    for k in range(4):
        first_leg(k).wait_recv()
        second_leg(k).start()
    for k in range(4):
        direct(1, k).wait_recv()
        direct(3, k).wait_recv()
        second_leg(k).wait_recv()

        def deliver(i, carry):
            j = (x + order[k]) % RING * 2 + i
            stage[j] = joined(j)

            @pl.when(j != head)
            def _():
                out_copy(j, head).start()

            @pl.when(j == head)
            def _():
                out_ref[head] = stage[j]

            return carry

        lax.fori_loop(0, 2, deliver, 0)

    for d in range(1, HEADS):
        out_copy((head + d) % HEADS, (head + d) % HEADS).wait_recv()
    for d in range(1, HEADS):
        out_copy((head + d) % HEADS, head).wait_send()
    for k in range(4):
        direct(1, k).wait_send()
        direct(3, k).wait_send()
        first_leg(k).wait_send()
        second_leg(k).wait_send()


def join(near_part, part):
    return pl.pallas_call(
        join_kernel,
        out_shape=jax.ShapeDtypeStruct((HEADS, HDIM, ROWS), BF16),
        in_specs=[VMEM, VMEM],
        out_specs=VMEM,
        scratch_shapes=[
            pltpu.VMEM((3, CL, BLOCK, BLOCK), BF16),
            pltpu.VMEM((4, PIECE, BLOCK, BLOCK), BF16),
            pltpu.VMEM((HEADS, HDIM, ROWS), BF16),
            pltpu.SemaphoreType.DMA((16,)),
            pltpu.SemaphoreType.DMA((16,)),
            pltpu.SemaphoreType.DMA((HEADS,)),
            pltpu.SemaphoreType.DMA((HEADS,)),
        ],
        compiler_params=pltpu.CompilerParams(
            collective_id=2, has_side_effects=True, vmem_limit_bytes=24 * 1024 * 1024
        ),
    )(pinned(near_part), pinned(part))


def tile_positions(tile_cols):
    line, head, z, y, core = place()
    mine = lax.dynamic_slice_in_dim(tile_cols, line * CL, CL, 0)[:, :LOC] - line * CL
    grid = tile_cols[:, LOC:].reshape(RING, RING, CL, FAR)
    along_y = lax.dynamic_index_in_dim(grid, z, 0, keepdims=False)
    along_z = lax.dynamic_index_in_dim(grid, y, 1, keepdims=False)
    cols = jnp.where(core == 0, along_y, along_z).reshape(QROWS, FAR)
    slab, within = cols // CL, cols % CL
    slab_z, slab_y = slab // RING, slab % RING
    here = jnp.where(core == 0, slab_y == y, slab_z == z) & (cols >= 0)
    index = jnp.where(core == 0, slab_z, slab_y)
    return mine, jnp.where(here, index * CL + within, -1)


def body(features, node_order, tile_cols, norm_gain, w_query, w_key, w_value, w_out):
    mine, pos = tile_positions(tile_cols)
    kvt, qt, near_part = near(
        features,
        norm_gain.reshape(1, D),
        node_order.reshape(1, SLAB),
        mine,
        w_query,
        w_key,
        w_value,
    )
    part = far(pos, kvt.reshape(QROWS, 2 * HDIM, BLOCK), qt.reshape(QROWS, HDIM, BLOCK))
    merged = join(near_part, part.reshape(RING, CL, BLOCK, BLOCK))
    return lax.dot_general(
        merged.reshape(D, ROWS), w_out, (((0,), (0,)), ((), ())), preferred_element_type=F32
    ).astype(BF16)


def solution(mesh):
    in_specs = (P(("loop", "head"), None), P("loop"), P(), P(), P(), P(), P(), P())
    out_specs = P(("loop", "head"), None)
    return jax.shard_map(body, mesh=mesh, in_specs=in_specs, out_specs=out_specs, check_vma=False)
```

```python
import functools
import math

import jax
import jax.numpy as jnp
from jax import lax
from jax.experimental import pallas as pl
from jax.experimental.pallas import tpu as pltpu
from jax.sharding import PartitionSpec as P

HEADS = 8
HDIM = 96
D = 768
BLOCK = 128
CL = 24
LOC = 21
FAR = 8
ROWS = 384
SLAB = 3072
RING = 4
QROWS = RING * CL
SCALE2 = math.log2(math.e) / math.sqrt(HDIM)
MESH = pl.DeviceIdType.MESH
VMEM = pl.BlockSpec(memory_space=pltpu.VMEM)
SMEM = pl.BlockSpec(memory_space=pltpu.SMEM)
ANY = pl.BlockSpec(memory_space=pl.ANY)
LIMIT = 58 * 1024 * 1024
NEG = -1e30
F32 = jnp.float32
BF16 = jnp.bfloat16
KEYS, VALUES, QUERIES = 0, 1, 2
HALF = CL // 2
CHUNK = 512
CHUNKS = SLAB // CHUNK
PIECE = 6
NEAR_GROUP = 4
NEAR_PAIRS = LOC // 2
FAR_PAIRS = FAR // 2
SUM_LOW, TOP_HIGH, TOP_MID, TOP_LOW = 104, 112, 118, 123


def nt(a, b):
    return lax.dot_general(a, b, (((1,), (1,)), ((), ())), preferred_element_type=F32)


def nn(a, b):
    return jnp.dot(a, b, preferred_element_type=F32)


def place():
    line = lax.axis_index("loop")
    head = lax.axis_index("head")
    z, y, core = line // RING, line % RING, head % 2
    return line, head, z, y, core


def on_kv_ring(step):
    line, head, z, y, core = place()
    return ((z + step * (1 - core)) % RING * RING + (y + step * core) % RING, head)


def on_q_ring(step):
    line, head, z, y, core = place()
    return ((z + step * core) % RING * RING + (y + step * (1 - core)) % RING, head)


def remote(src, dst, send, recv, device):
    return pltpu.make_async_remote_copy(
        src_ref=src,
        dst_ref=dst,
        send_sem=send,
        recv_sem=recv,
        device_id=device,
        device_id_type=MESH,
    )


def head_exchange(m, own, got, relay, send, recv):
    line, head, z, y, core = place()
    x = head // 2
    own, got, relay = own.at[m], got.at[m], relay.at[m]

    def to(step, c):
        return (x + step) % RING * 2 + c

    def direct(k, target):
        return remote(
            own.at[target], got.at[head], send.at[m, k], recv.at[m, head], (line, target)
        )

    def first_leg(c):
        step = 1 if c == 0 else 3
        return remote(
            own.at[to(2, c)],
            relay.at[c],
            send.at[m, 5 + c],
            recv.at[m, HEADS + c],
            (line, to(step, core)),
        )

    def second_leg(c):
        step = 1 if c == 0 else 3
        source = to(4 - step, core)
        return remote(
            relay.at[c],
            got.at[source],
            send.at[m, 7 + c],
            recv.at[m, source],
            (line, to(step, c)),
        )

    def arrived(source):
        remote(
            own.at[source], got.at[source], send.at[m, 0], recv.at[m, source], (line, source)
        ).wait_recv()

    targets = [to(0, 1 - core), to(1, 0), to(1, 1), to(3, 0), to(3, 1)]

    def start():
        for c in range(2):
            first_leg(c).start()
        for k in (1, 3, 2, 4, 0):
            direct(k, targets[k]).start()

    def forward():
        for c in range(2):
            first_leg(c).wait_recv()
            second_leg(c).start()

    def finish():
        for source in targets + [to(2, 0), to(2, 1)]:
            arrived(source)

    def drain():
        for k in range(5):
            direct(k, targets[k]).wait_send()
        for c in range(2):
            first_leg(c).wait_send()
            second_leg(c).wait_send()

    return start, forward, finish, drain


def ring_copies(m, own, table, pos, device, send, recv):
    before, after = (pos + RING - 1) % RING, (pos + 1) % RING
    plan = [
        (None, HALF, 1),
        (None, 0, 1),
        (None, 0, RING - 1),
        (None, HALF, RING - 1),
        (before, HALF, 1),
        (after, 0, RING - 1),
    ]

    def copy(k):
        block, start, step = plan[k]
        if block is None:
            src = own.at[pl.ds(start, HALF)]
            block = pos
        else:
            src = table.at[pl.ds(block * CL + start, HALF)]
        dst = table.at[pl.ds(block * CL + start, HALF)]
        return remote(src, dst, send.at[m, k], recv.at[m, k], device(step))

    return copy


def softmax_sums(queries, keys_of, values_of, pairs, s_scr, last=None, biases=None):
    group = range(len(queries))
    ones = jnp.ones((BLOCK - HDIM, 2 * BLOCK), BF16)
    tops = [None] * len(queries)
    for p in range(pairs):
        for u in group:
            score = nn(queries[u], keys_of(u, p))
            if biases is not None:
                low, high = biases[u][p]
                score = jnp.concatenate([score[:, :BLOCK] + low, score[:, BLOCK:] + high], axis=1)
            s_scr[u * pairs + p] = score
            tops[u] = score if p == 0 else jnp.maximum(tops[u], score)
    for u in group:
        tops[u] = jnp.maximum(tops[u][:, :BLOCK], tops[u][:, BLOCK:])
    if last is not None:
        ends = [nn(queries[u], last(u)[0]) for u in group]
        for u in group:
            tops[u] = jnp.maximum(tops[u], ends[u])
    for u in group:
        tops[u] = jnp.max(tops[u], axis=1, keepdims=True)
    totals = [None] * len(queries)
    if last is not None:
        for u in group:
            expo = jnp.exp2((ends[u] - tops[u]) * SCALE2).astype(BF16)
            totals[u] = nt(expo, jnp.concatenate([last(u)[1], ones[:, :BLOCK]], axis=0))
    for p in range(pairs):
        for u in group:
            expo = jnp.exp2((s_scr[u * pairs + p] - tops[u]) * SCALE2).astype(BF16)
            total = nt(expo, jnp.concatenate([values_of(u, p), ones], axis=0))
            totals[u] = total if totals[u] is None else totals[u] + total
    return totals, tops


def turned(block):
    return jnp.transpose(block.astype(F32)).astype(BF16)


def packed(total, top):
    lane = lax.broadcasted_iota(jnp.int32, total.shape, 1)
    return jnp.where(lane >= TOP_HIGH, top, total)


def in_parts(value):
    lane = lax.broadcasted_iota(jnp.int32, value.shape, 1)
    is_mid = ((lane >= SUM_LOW) & (lane < TOP_HIGH)) | ((lane >= TOP_MID) & (lane < TOP_LOW))
    high = value.astype(BF16).astype(F32)
    rest = value - high
    mid = rest.astype(BF16).astype(F32)
    return jnp.where(is_mid, mid, jnp.where(lane >= TOP_LOW, rest - mid, high)).astype(BF16)


def layer_kernel(
    feat_ref,
    gain_ref,
    order_ref,
    tiles_ref,
    wk_ref,
    wv_ref,
    wq_ref,
    out_ref,
    w_scr,
    wt_scr,
    proj,
    got,
    relay,
    pick_scr,
    own,
    kt,
    vt,
    qt,
    near_scr,
    far_scr,
    s_scr,
    part,
    back,
    turn,
    stage,
    w_sem,
    x_send,
    x_recv,
    ring_send,
    ring_recv,
    b_send,
    b_recv,
    o_send,
    o_recv,
):
    line, head, z, y, core = place()
    x = head // 2
    kv_pos = z * (1 - core) + y * core
    q_pos = z * core + y * (1 - core)
    loads = [
        pltpu.make_async_copy(ref, w_scr.at[m], w_sem.at[m])
        for m, ref in enumerate((wk_ref, wv_ref, wq_ref))
    ]
    for load in loads:
        load.start()
    partners = [on_kv_ring(1), on_kv_ring(3), on_q_ring(1), on_q_ring(3)]
    partners += [(line, (head + d) % HEADS) for d in range(1, HEADS)]
    barrier = pltpu.get_barrier_semaphore()
    for partner in partners:
        pl.semaphore_signal(barrier, inc=1, device_id=partner, device_id_type=MESH)

    wide = feat_ref[...].astype(F32)
    meansq = jnp.mean(wide * wide, axis=-1, keepdims=True)
    normed = (wide * lax.rsqrt(meansq + 1e-06) * gain_ref[...]).astype(BF16)
    exchanges = [head_exchange(m, proj, got, relay, x_send, x_recv) for m in range(3)]
    unit = jnp.where(
        lax.broadcasted_iota(jnp.int32, (D, D), 0) == lax.broadcasted_iota(jnp.int32, (D, D), 1),
        1.0,
        0.0,
    ).astype(BF16)

    def project(m):
        loads[m].wait()
        wt_scr[...] = nt(unit, w_scr[m]).astype(BF16)
        done = nt(wt_scr[...], normed).astype(BF16)
        for h in range(HEADS):
            proj[m, h] = done[h * HDIM : (h + 1) * HDIM]

    def picker(c, carry):
        every = lax.broadcasted_iota(jnp.int32, (SLAB, CHUNK), 0)
        order = order_ref[:, pl.ds(pl.multiple_of(c * CHUNK, CHUNK), CHUNK)]
        pick_scr[c] = jnp.where(every == order, 1.0, 0.0).astype(BF16)
        return carry

    def move(m, first, last):
        def step(c, carry):
            rows = jnp.concatenate([got[m, b] for b in range(HEADS)], axis=1)
            moved = nn(rows, pick_scr[c]).astype(BF16)
            for i in range(CHUNK // BLOCK):
                own[m, c * (CHUNK // BLOCK) + i] = moved[:, i * BLOCK : (i + 1) * BLOCK]
            return carry

        lax.fori_loop(first, last, step, 0)

    tables = (kt, vt, qt)
    rings = [
        ring_copies(
            m,
            own.at[m],
            tables[m],
            q_pos if m == QUERIES else kv_pos,
            on_q_ring if m == QUERIES else on_kv_ring,
            ring_send,
            ring_recv,
        )
        for m in range(3)
    ]

    def reorder_and_send(m):
        got[m, head] = proj[m, head]
        exchanges[m][2]()
        move(m, 0, CHUNKS // 2)
        rings[m](2).start()
        rings[m](1).start()
        move(m, CHUNKS // 2, CHUNKS)
        rings[m](0).start()
        rings[m](3).start()

    def pass_on(m, k):
        rings[m](k).wait_recv()
        rings[m](5 if k == 2 else 4).start()

    project(KEYS)
    pl.semaphore_wait(barrier, len(partners))
    exchanges[KEYS][0]()
    project(VALUES)
    exchanges[VALUES][0]()
    exchanges[KEYS][1]()
    project(QUERIES)
    exchanges[QUERIES][0]()
    lax.fori_loop(0, CHUNKS, picker, 0)
    exchanges[VALUES][1]()
    reorder_and_send(KEYS)
    exchanges[QUERIES][1]()
    pass_on(KEYS, 2)
    reorder_and_send(VALUES)
    pass_on(KEYS, 0)
    reorder_and_send(QUERIES)
    pass_on(VALUES, 2)
    for m in range(3):
        pos = q_pos if m == QUERIES else kv_pos
        tables[m][pl.ds(pos * CL, CL)] = own[m]

    def near(first, last):
        def step(g, carry):
            group = range(NEAR_GROUP)
            at = [g * NEAR_GROUP + u for u in group]
            cols = [[tiles_ref[q_pos * CL + c, t] for t in range(LOC)] for c in at]

            def joint(m):
                return lambda u, p: jnp.concatenate(
                    [own[m, cols[u][2 * p]], own[m, cols[u][2 * p + 1]]], axis=1
                )

            totals, tops = softmax_sums(
                [turned(own[QUERIES, c]) for c in at],
                joint(KEYS),
                joint(VALUES),
                NEAR_PAIRS,
                s_scr,
                last=lambda u: (own[KEYS, cols[u][LOC - 1]], own[VALUES, cols[u][LOC - 1]]),
            )
            for u in group:
                near_scr[at[u]] = packed(totals[u], tops[u])
            return carry

        lax.fori_loop(first, last, step, 0)

    near(0, 2)
    pass_on(VALUES, 0)
    pass_on(QUERIES, 2)
    near(2, 4)
    pass_on(QUERIES, 0)
    near(4, CL // NEAR_GROUP)
    for m in range(3):
        for k in (1, 3, 4, 5):
            rings[m](k).wait_recv()


    def far(block, first):
        group = range(PIECE)
        at = [block * CL + first + u for u in group]
        cols = [[tiles_ref[c, LOC + t] for t in range(FAR)] for c in at]
        safe = [[jnp.maximum(t, 0) for t in one] for one in cols]
        bias = [[jnp.where(t >= 0, 0.0, NEG) for t in one] for one in cols]

        def joint(table):
            return lambda u, p: jnp.concatenate(
                [table[safe[u][2 * p]], table[safe[u][2 * p + 1]]], axis=1
            )

        totals, tops = softmax_sums(
            [turned(qt[c]) for c in at],
            joint(kt),
            joint(vt),
            FAR_PAIRS,
            s_scr,
            biases=[[(one[2 * p], one[2 * p + 1]) for p in range(FAR_PAIRS)] for one in bias],
        )
        return [packed(total, top) for total, top in zip(totals, tops)]


    def first_row(k):
        return (x + 3 - k) % RING * PIECE

    def rows(k):
        return pl.ds(first_row(k), PIECE)

    def back_copy(src, dst, k, step):
        return remote(src, dst, b_send.at[k], b_recv.at[k], on_q_ring(step))

    def direct(way, k):
        step = 1 + 2 * way
        src = part.at[(q_pos + step) % RING, rows(k)]
        return back_copy(src, back.at[way, rows(k)], 4 * way + k, step)

    def first_leg(k):
        return back_copy(
            part.at[(q_pos + 2) % RING, rows(k)], turn.at[k], 8 + k, 1 + 2 * (k % 2)
        )

    def second_leg(k):
        return back_copy(turn.at[k], back.at[2, rows(k)], 12 + k, 1 + 2 * (k % 2))

    def far_part(step, k):
        block = (q_pos + step) % RING
        for u, one in enumerate(far(block, first_row(k))):
            part[block, first_row(k) + u] = in_parts(one)

    def opposite(k, carry):
        far_part(2, k)
        first_leg(k).start()
        return carry

    def neighbours(k, carry):
        far_part(1, k)
        direct(0, k).start()
        first_leg(k).wait_recv()
        second_leg(k).start()
        far_part(3, k)
        direct(1, k).start()
        return carry

    spread_row = lax.broadcasted_iota(jnp.int32, (BLOCK, 2 * BLOCK), 0)
    spread_col = lax.broadcasted_iota(jnp.int32, (BLOCK, 2 * BLOCK), 1)
    is_top = (spread_row == TOP_HIGH) | (spread_row == TOP_MID) | (spread_row == TOP_LOW)
    is_sum = (spread_row == HDIM) | (spread_row == SUM_LOW)
    spread = jnp.where(
        spread_col < BLOCK, jnp.where(is_top, 1.0, 0.0), jnp.where(is_sum, 1.0, 0.0)
    ).astype(BF16)

    def joined(c, i):
        sent = [back[way, c] for way in range(3)]
        both = nn(jnp.concatenate(sent, axis=0), spread)
        mine = [near_scr[c], far_scr[i]]
        values = mine + [one.astype(F32) for one in sent]
        tops = [jnp.broadcast_to(one[:, 127:128], (BLOCK, BLOCK)) for one in mine]
        sums = [jnp.broadcast_to(one[:, HDIM : HDIM + 1], (BLOCK, BLOCK)) for one in mine]
        for g in range(3):
            tops.append(both[g * BLOCK : (g + 1) * BLOCK, :BLOCK])
            sums.append(both[g * BLOCK : (g + 1) * BLOCK, BLOCK:])
        top = functools.reduce(jnp.maximum, tops)
        scales = [jnp.exp2((one - top) * SCALE2) for one in tops]
        whole = sum(a * b for a, b in zip(sums, scales))
        total = sum(a * b for a, b in zip(values, scales)) / whole
        return jnp.transpose(total)[:HDIM].astype(BF16)

    def out_copy(j, sender):
        return remote(
            stage.at[j], out_ref.at[sender], o_send.at[j], o_recv.at[sender], (line, j)
        )

    def close(k, carry):
        for u, one in enumerate(far(q_pos, first_row(k))):
            far_scr[u] = one
        direct(0, k).wait_recv()
        direct(1, k).wait_recv()
        second_leg(k).wait_recv()
        for i in range(2):
            j = first_row(k) // 3 + i
            stage[j] = jnp.concatenate([joined(j * 3 + c, i * 3 + c) for c in range(3)], axis=1)

            @pl.when(j != head)
            def _():
                out_copy(j, head).start()

            @pl.when(j == head)
            def _():
                out_ref[head] = stage[j]

        return carry

    lax.fori_loop(0, RING, opposite, 0)
    lax.fori_loop(0, RING, neighbours, 0)
    lax.fori_loop(0, RING, close, 0)

    for d in range(1, HEADS):
        out_copy((head + d) % HEADS, (head + d) % HEADS).wait_recv()
    for d in range(1, HEADS):
        out_copy((head + d) % HEADS, head).wait_send()
    for k in range(RING):
        direct(0, k).wait_send()
        direct(1, k).wait_send()
        first_leg(k).wait_send()
        second_leg(k).wait_send()
    for m in range(3):
        exchanges[m][3]()
        for k in range(6):
            rings[m](k).wait_send()


def layer(features, gain, order, tiles, wk, wv, wq):
    dma = pltpu.SemaphoreType.DMA
    return pl.pallas_call(
        layer_kernel,
        out_shape=jax.ShapeDtypeStruct((HEADS, HDIM, ROWS), BF16),
        in_specs=[VMEM, VMEM, VMEM, SMEM, ANY, ANY, ANY],
        out_specs=VMEM,
        scratch_shapes=[
            pltpu.VMEM((3, D, D), BF16),
            pltpu.VMEM((D, D), BF16),
            pltpu.VMEM((3, HEADS, HDIM, ROWS), BF16),
            pltpu.VMEM((3, HEADS, HDIM, ROWS), BF16),
            pltpu.VMEM((3, 2, HDIM, ROWS), BF16),
            pltpu.VMEM((CHUNKS, SLAB, CHUNK), BF16),
            pltpu.VMEM((3, CL, HDIM, BLOCK), BF16),
            pltpu.VMEM((QROWS, HDIM, BLOCK), BF16),
            pltpu.VMEM((QROWS, HDIM, BLOCK), BF16),
            pltpu.VMEM((QROWS, HDIM, BLOCK), BF16),
            pltpu.VMEM((CL, BLOCK, BLOCK), F32),
            pltpu.VMEM((PIECE, BLOCK, BLOCK), F32),
            pltpu.VMEM((NEAR_GROUP * NEAR_PAIRS, BLOCK, 2 * BLOCK), F32),
            pltpu.VMEM((RING, CL, BLOCK, BLOCK), BF16),
            pltpu.VMEM((3, CL, BLOCK, BLOCK), BF16),
            pltpu.VMEM((RING, PIECE, BLOCK, BLOCK), BF16),
            pltpu.VMEM((HEADS, HDIM, ROWS), BF16),
            dma((3,)),
            dma((3, 9)),
            dma((3, HEADS + 2)),
            dma((3, 6)),
            dma((3, 6)),
            dma((4 * RING,)),
            dma((4 * RING,)),
            dma((HEADS,)),
            dma((HEADS,)),
        ],
        compiler_params=pltpu.CompilerParams(
            collective_id=1, has_side_effects=True, vmem_limit_bytes=LIMIT
        ),
    )(features, gain, order, tiles, wk, wv, wq)


def tile_positions(tile_cols):
    line, head, z, y, core = place()
    grid = tile_cols.reshape(RING, RING, CL, LOC + FAR)
    along_y = lax.dynamic_index_in_dim(grid, z, 0, keepdims=False)
    along_z = lax.dynamic_index_in_dim(grid, y, 1, keepdims=False)
    cols = jnp.where(core == 0, along_y, along_z).reshape(QROWS, LOC + FAR)
    slab, within = cols // CL, cols % CL
    slab_z, slab_y = slab // RING, slab % RING
    here = jnp.where(core == 0, slab_y == y, slab_z == z) & (cols >= 0)
    index = jnp.where(core == 0, slab_z, slab_y)
    is_near = lax.broadcasted_iota(jnp.int32, cols.shape, 1) < LOC
    return jnp.where(is_near, within, jnp.where(here, index * CL + within, -1))


def body(features, node_order, tile_cols, norm_gain, w_query, w_key, w_value, w_out):
    merged = layer(
        features,
        norm_gain.reshape(1, D),
        node_order.reshape(1, SLAB),
        tile_positions(tile_cols),
        w_key,
        w_value,
        w_query,
    )
    return lax.dot_general(
        merged.reshape(D, ROWS), w_out, (((0,), (0,)), ((), ())), preferred_element_type=F32
    ).astype(BF16)


def solution(mesh):
    in_specs = (P(("loop", "head"), None), P("loop"), P(), P(), P(), P(), P(), P())
    out_specs = P(("loop", "head"), None)
    return jax.shard_map(body, mesh=mesh, in_specs=in_specs, out_specs=out_specs, check_vma=False)
```

```python
import functools
import math

import jax
import jax.numpy as jnp
from jax import lax
from jax.experimental import pallas as pl
from jax.experimental.pallas import tpu as pltpu
from jax.sharding import PartitionSpec as P

HEADS = 8
HDIM = 96
D = 768
BLOCK = 128
CL = 24
LOC = 21
FAR = 8
ROWS = 384
SLAB = 3072
RING = 4
QROWS = RING * CL
SCALE2 = math.log2(math.e) / math.sqrt(HDIM)
MESH = pl.DeviceIdType.MESH
VMEM = pl.BlockSpec(memory_space=pltpu.VMEM)
SMEM = pl.BlockSpec(memory_space=pltpu.SMEM)
ANY = pl.BlockSpec(memory_space=pl.ANY)
LIMIT = 54 * 1024 * 1024
NEG = -1e30
F32 = jnp.float32
BF16 = jnp.bfloat16
KEYS, VALUES, QUERIES = 0, 1, 2
HALF = CL // 2
CHUNK = 256
CHUNKS = SLAB // CHUNK
PIECE = 6
NEAR_GROUP = 4
NEAR_PAIRS = LOC // 2
FAR_PAIRS = FAR // 2
STATS = 16
TALL = HDIM + STATS
SUM_LOW, TOP_HIGH, TOP_MID, TOP_LOW = 4, 8, 11, 14


def nt(a, b):
    return lax.dot_general(a, b, (((1,), (1,)), ((), ())), preferred_element_type=F32)


def nn(a, b):
    return jnp.dot(a, b, preferred_element_type=F32)


def place():
    line = lax.axis_index("loop")
    head = lax.axis_index("head")
    z, y, core = line // RING, line % RING, head % 2
    return line, head, z, y, core


def on_kv_ring(step):
    line, head, z, y, core = place()
    return ((z + step * (1 - core)) % RING * RING + (y + step * core) % RING, head)


def on_q_ring(step):
    line, head, z, y, core = place()
    return ((z + step * core) % RING * RING + (y + step * (1 - core)) % RING, head)


def remote(src, dst, send, recv, device):
    return pltpu.make_async_remote_copy(
        src_ref=src,
        dst_ref=dst,
        send_sem=send,
        recv_sem=recv,
        device_id=device,
        device_id_type=MESH,
    )


def head_exchange(m, own, got, send, recv):
    line, head, z, y, core = place()
    x = head // 2
    own, got = own.at[m], got.at[m]
    near = [x * 2 + 1 - core]
    near += [(x + step) % RING * 2 + c for step in (1, 3) for c in range(2)]
    opposite = [(x + 2) % RING * 2 + c for c in range(2)]

    def to(k, target):
        return remote(
            own.at[target], got.at[head], send.at[m, k], recv.at[m, head], (line, target)
        )

    def arrived(source):
        remote(
            own.at[source], got.at[source], send.at[m, 0], recv.at[m, source], (line, source)
        ).wait_recv()

    def start():
        for k, target in enumerate(opposite + near):
            to(k, target).start()

    def finish_near():
        for source in near:
            arrived(source)

    def finish():
        for source in opposite:
            arrived(source)

    def drain():
        for k, target in enumerate(opposite + near):
            to(k, target).wait_send()

    return start, finish_near, finish, drain


def ring_copies(m, own, table, pos, device, send, recv):
    before, after = (pos + RING - 1) % RING, (pos + 1) % RING
    plan = [
        (None, HALF, 1),
        (None, 0, 1),
        (None, 0, RING - 1),
        (None, HALF, RING - 1),
        (before, 0, 1),
        (after, HALF, RING - 1),
    ]

    def copy(k):
        block, start, step = plan[k]
        if block is None:
            src = own.at[pl.ds(start, HALF)]
            block = pos
        else:
            src = table.at[pl.ds(block * CL + start, HALF)]
        dst = table.at[pl.ds(block * CL + start, HALF)]
        return remote(src, dst, send.at[m, k], recv.at[m, k], device(step))

    return copy


def scores(queries, keys_of, pairs, s_scr, last=None, biases=None):
    group = range(len(queries))
    tops = [None] * len(queries)
    for p in range(pairs):
        for u in group:
            score = nn(queries[u], keys_of(u, p))
            if biases is not None:
                low, high = biases[u][p]
                score = jnp.concatenate([score[:, :BLOCK] + low, score[:, BLOCK:] + high], axis=1)
            s_scr[u * pairs + p] = score
            tops[u] = score if p == 0 else jnp.maximum(tops[u], score)
    for u in group:
        tops[u] = jnp.maximum(tops[u][:, :BLOCK], tops[u][:, BLOCK:])
    ends = None
    if last is not None:
        ends = [nn(queries[u], last(u)) for u in group]
        for u in group:
            tops[u] = jnp.maximum(tops[u], ends[u])
    return [jnp.max(top, axis=1, keepdims=True) for top in tops], ends


def exponent(score, top):
    return jnp.exp2((score - top) * SCALE2).astype(BF16)


def tall_sums(values, expo):
    ones = jnp.ones((STATS, values.shape[1]), BF16)
    return nt(jnp.concatenate([values, ones], axis=0), expo)


def across(top):
    lane = lax.broadcasted_iota(jnp.int32, (BLOCK, BLOCK), 1)
    top = jnp.broadcast_to(top, (BLOCK, BLOCK))
    high = top.astype(BF16).astype(F32)
    rest = top - high
    mid = rest.astype(BF16).astype(F32)
    parts = jnp.where(lane == 0, high, jnp.where(lane == 1, mid, rest - mid))
    parts = jnp.where(lane < 3, parts, 0.0).astype(BF16)
    return nt(jnp.ones((STATS, BLOCK), BF16), parts)


def with_stats(total, top_rows):
    row = lax.broadcasted_iota(jnp.int32, (STATS, BLOCK), 0)
    stats = jnp.where(row < TOP_HIGH, total[HDIM:], top_rows)
    return jnp.concatenate([total[:HDIM], stats], axis=0)


def in_parts(tall):
    row = lax.broadcasted_iota(jnp.int32, (STATS, BLOCK), 0)
    is_mid = ((row >= SUM_LOW) & (row < TOP_HIGH)) | ((row >= TOP_MID) & (row < TOP_LOW))
    stats = tall[HDIM:]
    high = stats.astype(BF16).astype(F32)
    rest = stats - high
    mid = rest.astype(BF16).astype(F32)
    stats = jnp.where(is_mid, mid, jnp.where(row >= TOP_LOW, rest - mid, high))
    return jnp.concatenate([tall[:HDIM].astype(BF16), stats.astype(BF16)], axis=0)


def turned(block):
    return jnp.transpose(block.astype(F32)).astype(BF16)


def layer_kernel(
    feat_ref,
    gain_ref,
    order_ref,
    tiles_ref,
    wk_ref,
    wv_ref,
    wq_ref,
    out_ref,
    order_scr,
    w_scr,
    wt_scr,
    proj,
    got,
    pick_scr,
    own,
    kt,
    vt,
    qt,
    near_scr,
    far_scr,
    s_scr,
    part,
    back,
    turn,
    stage,
    w_sem,
    x_send,
    x_recv,
    ring_send,
    ring_recv,
    b_send,
    b_recv,
    o_send,
    o_recv,
):
    line, head, z, y, core = place()
    x = head // 2
    kv_pos = z * (1 - core) + y * core
    q_pos = z * core + y * (1 - core)
    loads = [
        pltpu.make_async_copy(ref, w_scr.at[m], w_sem.at[m])
        for m, ref in enumerate((wk_ref, wv_ref, wq_ref))
    ]
    for load in loads:
        load.start()
    partners = [on_kv_ring(1), on_kv_ring(3), on_q_ring(1), on_q_ring(3)]
    partners += [(line, (head + d) % HEADS) for d in range(1, HEADS)]
    barrier = pltpu.get_barrier_semaphore()
    for partner in partners:
        pl.semaphore_signal(barrier, inc=1, device_id=partner, device_id_type=MESH)

    wide = feat_ref[...].astype(F32)
    meansq = jnp.mean(wide * wide, axis=-1, keepdims=True)
    normed = (wide * lax.rsqrt(meansq + 1e-06) * gain_ref[...][None, :]).astype(BF16)
    exchanges = [head_exchange(m, proj, got, x_send, x_recv) for m in range(3)]
    unit = jnp.where(
        lax.broadcasted_iota(jnp.int32, (D, D), 0) == lax.broadcasted_iota(jnp.int32, (D, D), 1),
        1.0,
        0.0,
    ).astype(BF16)

    def project(m):
        loads[m].wait()
        wt_scr[...] = nt(unit, w_scr[m]).astype(BF16)
        done = nt(wt_scr[...], normed).astype(BF16)
        for h in range(HEADS):
            proj[m, h] = done[h * HDIM : (h + 1) * HDIM]

    tall = SLAB // BLOCK

    def picker(c, carry):
        every = lax.broadcasted_iota(jnp.int32, (SLAB, CHUNK), 0)
        order = order_scr[:, pl.ds(pl.multiple_of(c * CHUNK, CHUNK), CHUNK)]
        pick = jnp.where(every == order, 1.0, 0.0).astype(BF16)
        pick_scr[pl.ds(c * tall, tall)] = pick.reshape(tall, BLOCK, CHUNK)
        return carry

    def move(m, first, last):
        def step(c, carry):
            rows = jnp.concatenate([got[m, b] for b in range(HEADS)], axis=1)
            pick = pick_scr[pl.ds(c * tall, tall)].reshape(SLAB, CHUNK)
            moved = nn(rows, pick).astype(BF16)
            for i in range(CHUNK // BLOCK):
                own[m, c * (CHUNK // BLOCK) + i] = moved[:, i * BLOCK : (i + 1) * BLOCK]
            return carry

        lax.fori_loop(first, last, step, 0)

    tables = (kt, vt, qt)
    rings = [
        ring_copies(
            m,
            own.at[m],
            tables[m],
            q_pos if m == QUERIES else kv_pos,
            on_q_ring if m == QUERIES else on_kv_ring,
            ring_send,
            ring_recv,
        )
        for m in range(3)
    ]

    def reorder_and_send(m, between=None):
        move(m, 0, CHUNKS // 2)
        rings[m](1).start()
        if between is not None:
            between()
        move(m, CHUNKS // 2, CHUNKS)
        rings[m](3).start()
        rings[m](0).start()
        rings[m](2).start()

    def pass_on(m, k):
        rings[m](k).wait_recv()
        rings[m](4 if k == 1 else 5).start()

    def received(m):
        for k in (0, 2, 4, 5):
            rings[m](k).wait_recv()

    def keep(m):
        got[m, head] = proj[m, head]

    def begin(m):
        exchanges[m][0]()

    def finish_near(m):
        exchanges[m][1]()

    def finish(m):
        exchanges[m][2]()

    project(KEYS)
    pl.semaphore_wait(barrier, len(partners))
    begin(KEYS)
    project(QUERIES)
    project(VALUES)
    order_scr[...] = order_ref[...][None, :]
    lax.fori_loop(0, CHUNKS, picker, 0)
    for m in range(3):
        keep(m)
    finish_near(KEYS)
    begin(QUERIES)
    finish(KEYS)
    reorder_and_send(KEYS)
    finish_near(QUERIES)
    begin(VALUES)
    finish(QUERIES)
    pass_on(KEYS, 1)
    reorder_and_send(QUERIES, lambda: pass_on(KEYS, 3))
    finish_near(VALUES)
    finish(VALUES)
    reorder_and_send(VALUES, lambda: pass_on(QUERIES, 1))
    pass_on(QUERIES, 3)
    for m in range(3):
        pos = q_pos if m == QUERIES else kv_pos
        tables[m][pl.ds(pos * CL, CL)] = own[m]

    def near(g):
        group = range(NEAR_GROUP)
        at = [g * NEAR_GROUP + u for u in group]
        cols = [[tiles_ref[q_pos * CL + c, t] for t in range(LOC)] for c in at]

        def joint(m):
            return lambda u, p: jnp.concatenate(
                [own[m, cols[u][2 * p]], own[m, cols[u][2 * p + 1]]], axis=1
            )

        queries = [turned(own[QUERIES, c]) for c in at]
        tops, ends = scores(
            queries, joint(KEYS), NEAR_PAIRS, s_scr, last=lambda u: own[KEYS, cols[u][LOC - 1]]
        )
        totals = [
            tall_sums(own[VALUES, cols[u][LOC - 1]], exponent(ends[u], tops[u])) for u in group
        ]
        for p in range(NEAR_PAIRS):
            for u in group:
                expo = exponent(s_scr[u * NEAR_PAIRS + p], tops[u])
                totals[u] += tall_sums(joint(VALUES)(u, p), expo)
        for u in group:
            near_scr[at[u]] = with_stats(totals[u], across(tops[u]))


    def far_tiles(at):
        cols = [[tiles_ref[c, LOC + t] for t in range(FAR)] for c in at]
        return cols, [[jnp.maximum(t, 0) for t in one] for one in cols]

    def joint_far(table, safe):
        return lambda u, p: jnp.concatenate(
            [table[safe[u][2 * p]], table[safe[u][2 * p + 1]]], axis=1
        )

    def far_scores(at):
        cols, safe = far_tiles(at)
        bias = [[jnp.where(t >= 0, 0.0, NEG) for t in one] for one in cols]
        return scores(
            [turned(qt[c]) for c in at],
            joint_far(kt, safe),
            FAR_PAIRS,
            s_scr,
            biases=[[(one[2 * p], one[2 * p + 1]) for p in range(FAR_PAIRS)] for one in bias],
        )[0]

    def far_rows(step, k):
        block = (q_pos + step) % RING
        return block, [block * CL + first_row(k) + u for u in range(PIECE)]

    def far_results(step, k):
        at = far_rows(step, k)[1] + far_rows(step, k + 1)[1]
        tops = far_scores(at)
        values = joint_far(vt, far_tiles(at)[1])
        totals = [None] * len(at)
        for p in range(FAR_PAIRS):
            for u in range(len(at)):
                expo = exponent(s_scr[u * FAR_PAIRS + p], tops[u])
                total = tall_sums(values(u, p), expo)
                totals[u] = total if p == 0 else totals[u] + total
        return [with_stats(total, across(top)) for total, top in zip(totals, tops)]

    def far_part(step, k):
        block = (q_pos + step) % RING
        for u, one in enumerate(far_results(step, k)):
            part[block, first_row(k + u // PIECE) + u % PIECE] = in_parts(one)


    def first_row(k):
        return (x + 3 - k) % RING * PIECE

    def rows(k):
        return pl.ds(first_row(k), PIECE)

    def back_copy(src, dst, k, step):
        return remote(src, dst, b_send.at[k], b_recv.at[k], on_q_ring(step))

    def direct(way, k):
        step = 1 + 2 * way
        src = part.at[(q_pos + step) % RING, rows(k)]
        return back_copy(src, back.at[way, rows(k)], 4 * way + k, step)

    def first_leg(k):
        return back_copy(
            part.at[(q_pos + 2) % RING, rows(k)], turn.at[k], 8 + k, 1 + 2 * (k % 2)
        )

    def second_leg(k):
        return back_copy(turn.at[k], back.at[2, rows(k)], 12 + k, 1 + 2 * (k % 2))

    def opposite(i, carry):
        far_part(2, 2 * i)
        first_leg(2 * i).start()
        first_leg(2 * i + 1).start()
        return carry

    def neighbours(i, carry):
        far_part(1, 2 * i)
        direct(0, 2 * i).start()
        direct(0, 2 * i + 1).start()
        for k in (2 * i, 2 * i + 1):
            first_leg(k).wait_recv()
            second_leg(k).start()
        far_part(3, 2 * i)
        direct(1, 2 * i).start()
        direct(1, 2 * i + 1).start()
        return carry

    def own_far(i, carry):
        for u, one in enumerate(far_results(0, 2 * i)):
            far_scr[i * 2 * PIECE + u] = one
        return carry

    def joined(c, i):
        values, tops, sums = [], [], []
        for tall_result in (near_scr[c], far_scr[i]):
            values.append(tall_result[:HDIM])
            sums.append(tall_result[HDIM : HDIM + 1])
            tops.append(tall_result[HDIM + TOP_HIGH : HDIM + TOP_HIGH + 1])
        for way in range(3):
            sent = back[way, c].astype(F32)
            values.append(sent[:HDIM])
            stat = [sent[HDIM + r : HDIM + r + 1] for r in range(STATS)]
            sums.append(stat[0] + stat[SUM_LOW])
            tops.append(stat[TOP_HIGH] + stat[TOP_MID] + stat[TOP_LOW])
        top = functools.reduce(jnp.maximum, tops)
        scales = [jnp.exp2((one - top) * SCALE2) for one in tops]
        whole = sum(a * b for a, b in zip(sums, scales))
        scales = [one / whole for one in scales]
        return sum(a * b for a, b in zip(values, scales)).astype(BF16)

    def out_copy(j, sender):
        return remote(
            stage.at[j], out_ref.at[sender], o_send.at[j], o_recv.at[sender], (line, j)
        )

    def close(k, carry):
        direct(0, k).wait_recv()
        direct(1, k).wait_recv()
        second_leg(k).wait_recv()
        for i in range(2):
            j = first_row(k) // 3 + i
            stage[j] = jnp.concatenate([joined(j * 3 + c, k * PIECE + i * 3 + c) for c in range(3)], axis=1)

            @pl.when(j != head)
            def _():
                out_copy(j, head).start()

            @pl.when(j == head)
            def _():
                out_ref[head] = stage[j]

        return carry

    def some_near(first, last):
        def one(g, carry):
            near(g)
            return carry

        lax.fori_loop(first, last, one, 0)

    some_near(0, 2)
    pass_on(VALUES, 1)
    some_near(2, 3)
    pass_on(VALUES, 3)
    some_near(3, CL // NEAR_GROUP)
    for m in range(3):
        received(m)
    lax.fori_loop(0, 2, opposite, 0)
    lax.fori_loop(0, 2, neighbours, 0)
    lax.fori_loop(0, 2, own_far, 0)
    lax.fori_loop(0, RING, close, 0)

    for d in range(1, HEADS):
        out_copy((head + d) % HEADS, (head + d) % HEADS).wait_recv()
    for d in range(1, HEADS):
        out_copy((head + d) % HEADS, head).wait_send()
    for k in range(RING):
        direct(0, k).wait_send()
        direct(1, k).wait_send()
        first_leg(k).wait_send()
        second_leg(k).wait_send()
    for m in range(3):
        exchanges[m][3]()
        for k in range(6):
            rings[m](k).wait_send()


def layer(features, gain, order, tiles, wk, wv, wq):
    dma = pltpu.SemaphoreType.DMA
    return pl.pallas_call(
        layer_kernel,
        out_shape=pltpu.VMEM((HEADS, HDIM, ROWS), BF16),
        in_specs=[VMEM, VMEM, VMEM, SMEM, ANY, ANY, ANY],
        out_specs=VMEM,
        scratch_shapes=[
            pltpu.VMEM((1, SLAB), jnp.int32),
            pltpu.VMEM((3, D, D), BF16),
            pltpu.VMEM((D, D), BF16),
            pltpu.VMEM((3, HEADS, HDIM, ROWS), BF16),
            pltpu.VMEM((3, HEADS, HDIM, ROWS), BF16),
            pltpu.VMEM((CHUNKS * (SLAB // BLOCK), BLOCK, CHUNK), BF16),
            pltpu.VMEM((3, CL, HDIM, BLOCK), BF16),
            pltpu.VMEM((QROWS, HDIM, BLOCK), BF16),
            pltpu.VMEM((QROWS, HDIM, BLOCK), BF16),
            pltpu.VMEM((QROWS, HDIM, BLOCK), BF16),
            pltpu.VMEM((CL, TALL, BLOCK), F32),
            pltpu.VMEM((CL, TALL, BLOCK), F32),
            pltpu.VMEM((2 * PIECE * FAR_PAIRS, BLOCK, 2 * BLOCK), F32),
            pltpu.VMEM((RING, CL, TALL, BLOCK), BF16),
            pltpu.VMEM((3, CL, TALL, BLOCK), BF16),
            pltpu.VMEM((RING, PIECE, TALL, BLOCK), BF16),
            pltpu.VMEM((HEADS, HDIM, ROWS), BF16),
            dma((3,)),
            dma((3, HEADS)),
            dma((3, HEADS)),
            dma((3, 6)),
            dma((3, 6)),
            dma((4 * RING,)),
            dma((4 * RING,)),
            dma((HEADS,)),
            dma((HEADS,)),
        ],
        compiler_params=pltpu.CompilerParams(
            collective_id=1, has_side_effects=True, vmem_limit_bytes=LIMIT
        ),
    )(features, gain, order, tiles, wk, wv, wq)


def tile_positions(tile_cols):
    line, head, z, y, core = place()
    grid = tile_cols.reshape(RING, RING, CL, LOC + FAR)
    along_y = lax.dynamic_index_in_dim(grid, z, 0, keepdims=False)
    along_z = lax.dynamic_index_in_dim(grid, y, 1, keepdims=False)
    cols = jnp.where(core == 0, along_y, along_z).reshape(QROWS, LOC + FAR)
    slab, within = cols // CL, cols % CL
    slab_z, slab_y = slab // RING, slab % RING
    here = jnp.where(core == 0, slab_y == y, slab_z == z) & (cols >= 0)
    index = jnp.where(core == 0, slab_z, slab_y)
    is_near = lax.broadcasted_iota(jnp.int32, cols.shape, 1) < LOC
    return jnp.where(is_near, within, jnp.where(here, index * CL + within, -1))


def body(features, node_order, tile_cols, norm_gain, w_query, w_key, w_value, w_out):
    merged = layer(
        features,
        norm_gain,
        node_order,
        tile_positions(tile_cols),
        w_key,
        w_value,
        w_query,
    )
    return lax.dot_general(
        merged.reshape(D, ROWS), w_out, (((0,), (0,)), ((), ())), preferred_element_type=F32
    ).astype(BF16)


def solution(mesh):
    in_specs = (P(("loop", "head"), None), P("loop"), P(), P(), P(), P(), P(), P())
    out_specs = P(("loop", "head"), None)
    return jax.shard_map(body, mesh=mesh, in_specs=in_specs, out_specs=out_specs, check_vma=False)
```

```python
import functools
import math

import jax
import jax.numpy as jnp
from jax import lax
from jax.experimental import pallas as pl
from jax.experimental.pallas import tpu as pltpu
from jax.sharding import PartitionSpec as P

HEADS = 8
HDIM = 96
D = 768
BLOCK = 128
CL = 24
LOC = 21
FAR = 8
ROWS = 384
SLAB = 3072
RING = 4
QROWS = RING * CL
SCALE2 = math.log2(math.e) / math.sqrt(HDIM)
MESH = pl.DeviceIdType.MESH
VMEM = pl.BlockSpec(memory_space=pltpu.VMEM)
SMEM = pl.BlockSpec(memory_space=pltpu.SMEM)
ANY = pl.BlockSpec(memory_space=pl.ANY)
LIMIT = 54 * 1024 * 1024
NEG = -1e30
F32 = jnp.float32
BF16 = jnp.bfloat16
KEYS, VALUES, QUERIES = 0, 1, 2
HALF = CL // 2
CHUNK = 256
CHUNKS = SLAB // CHUNK
PIECE = 6
NEAR_GROUP = 4
NEAR_PAIRS = LOC // 2
FAR_PAIRS = FAR // 2
STATS = 16
TALL = HDIM + STATS
SUM_LOW, TOP_HIGH, TOP_MID, TOP_LOW = 4, 8, 11, 14


def nt(a, b):
    return lax.dot_general(a, b, (((1,), (1,)), ((), ())), preferred_element_type=F32)


def nn(a, b):
    return jnp.dot(a, b, preferred_element_type=F32)


def place():
    line = lax.axis_index("loop")
    head = lax.axis_index("head")
    z, y, core = line // RING, line % RING, head % 2
    return line, head, z, y, core


def on_kv_ring(step):
    line, head, z, y, core = place()
    return ((z + step * (1 - core)) % RING * RING + (y + step * core) % RING, head)


def on_q_ring(step):
    line, head, z, y, core = place()
    return ((z + step * core) % RING * RING + (y + step * (1 - core)) % RING, head)


def remote(src, dst, send, recv, device):
    return pltpu.make_async_remote_copy(
        src_ref=src,
        dst_ref=dst,
        send_sem=send,
        recv_sem=recv,
        device_id=device,
        device_id_type=MESH,
    )


def head_exchange(m, own, got, send, recv):
    line, head, z, y, core = place()
    x = head // 2
    own, got = own.at[m], got.at[m]
    near = [x * 2 + 1 - core]
    near += [(x + step) % RING * 2 + c for step in (1, 3) for c in range(2)]
    opposite = [(x + 2) % RING * 2 + c for c in range(2)]

    def to(k, target):
        return remote(
            own.at[target], got.at[head], send.at[m, k], recv.at[m, head], (line, target)
        )

    def arrived(source):
        remote(
            own.at[source], got.at[source], send.at[m, 0], recv.at[m, source], (line, source)
        ).wait_recv()

    def start():
        for k, target in enumerate(opposite + near):
            to(k, target).start()

    def finish_near():
        for source in near:
            arrived(source)

    def finish():
        for source in opposite:
            arrived(source)

    def drain():
        for k, target in enumerate(opposite + near):
            to(k, target).wait_send()

    return start, finish_near, finish, drain


def ring_copies(m, own, table, pos, device, send, recv):
    before, after = (pos + RING - 1) % RING, (pos + 1) % RING
    plan = [
        (None, HALF, 1),
        (None, 0, 1),
        (None, 0, RING - 1),
        (None, HALF, RING - 1),
        (before, 0, 1),
        (after, HALF, RING - 1),
    ]

    def copy(k):
        block, start, step = plan[k]
        if block is None:
            src = own.at[pl.ds(start, HALF)]
            block = pos
        else:
            src = table.at[pl.ds(block * CL + start, HALF)]
        dst = table.at[pl.ds(block * CL + start, HALF)]
        return remote(src, dst, send.at[m, k], recv.at[m, k], device(step))

    return copy


def scores(queries, keys_of, pairs, s_scr, last=None, biases=None):
    group = range(len(queries))
    tops = [None] * len(queries)
    for p in range(pairs):
        for u in group:
            score = nn(queries[u], keys_of(u, p))
            if biases is not None:
                low, high = biases[u][p]
                score = jnp.concatenate([score[:, :BLOCK] + low, score[:, BLOCK:] + high], axis=1)
            s_scr[u * pairs + p] = score
            tops[u] = score if p == 0 else jnp.maximum(tops[u], score)
    for u in group:
        tops[u] = jnp.maximum(tops[u][:, :BLOCK], tops[u][:, BLOCK:])
    ends = None
    if last is not None:
        ends = [nn(queries[u], last(u)) for u in group]
        for u in group:
            tops[u] = jnp.maximum(tops[u], ends[u])
    return [jnp.max(top, axis=1, keepdims=True) for top in tops], ends


def exponent(score, top):
    return jnp.exp2((score - top) * SCALE2).astype(BF16)


def tall_sums(values, expo):
    ones = jnp.ones((STATS, values.shape[1]), BF16)
    return nt(jnp.concatenate([values, ones], axis=0), expo)


def across(top):
    lane = lax.broadcasted_iota(jnp.int32, (BLOCK, BLOCK), 1)
    top = jnp.broadcast_to(top, (BLOCK, BLOCK))
    high = top.astype(BF16).astype(F32)
    rest = top - high
    mid = rest.astype(BF16).astype(F32)
    parts = jnp.where(lane == 0, high, jnp.where(lane == 1, mid, rest - mid))
    parts = jnp.where(lane < 3, parts, 0.0).astype(BF16)
    return nt(jnp.ones((STATS, BLOCK), BF16), parts)


def with_stats(total, top_rows):
    row = lax.broadcasted_iota(jnp.int32, (STATS, BLOCK), 0)
    stats = jnp.where(row < TOP_HIGH, total[HDIM:], top_rows)
    return jnp.concatenate([total[:HDIM], stats], axis=0)


def in_parts(tall):
    row = lax.broadcasted_iota(jnp.int32, (STATS, BLOCK), 0)
    is_mid = ((row >= SUM_LOW) & (row < TOP_HIGH)) | ((row >= TOP_MID) & (row < TOP_LOW))
    stats = tall[HDIM:]
    high = stats.astype(BF16).astype(F32)
    rest = stats - high
    mid = rest.astype(BF16).astype(F32)
    stats = jnp.where(is_mid, mid, jnp.where(row >= TOP_LOW, rest - mid, high))
    return jnp.concatenate([tall[:HDIM].astype(BF16), stats.astype(BF16)], axis=0)


def turned(block):
    return jnp.transpose(block.astype(F32)).astype(BF16)


def layer_kernel(
    feat_ref,
    gain_ref,
    order_ref,
    tiles_ref,
    wk_ref,
    wv_ref,
    wq_ref,
    out_ref,
    order_scr,
    feat_scr,
    w_scr,
    wt_scr,
    proj,
    got,
    pick_scr,
    own,
    kt,
    vt,
    qt,
    near_scr,
    far_scr,
    s_scr,
    part,
    back,
    turn,
    stage,
    w_sem,
    x_send,
    x_recv,
    ring_send,
    ring_recv,
    b_send,
    b_recv,
    o_send,
    o_recv,
):
    line, head, z, y, core = place()
    x = head // 2
    kv_pos = z * (1 - core) + y * core
    q_pos = z * core + y * (1 - core)
    feat_load = pltpu.make_async_copy(feat_ref, feat_scr, w_sem.at[3])
    feat_load.start()
    loads = [
        pltpu.make_async_copy(ref, w_scr.at[m], w_sem.at[m])
        for m, ref in enumerate((wk_ref, wv_ref, wq_ref))
    ]
    for m in (KEYS, QUERIES, VALUES):
        loads[m].start()
    partners = [on_kv_ring(1), on_kv_ring(3), on_q_ring(1), on_q_ring(3)]
    partners += [(line, (head + d) % HEADS) for d in range(1, HEADS)]
    barrier = pltpu.get_barrier_semaphore()
    for partner in partners:
        pl.semaphore_signal(barrier, inc=1, device_id=partner, device_id_type=MESH)

    feat_load.wait()
    wide = feat_scr[...].astype(F32)
    meansq = jnp.mean(wide * wide, axis=-1, keepdims=True)
    normed = (wide * lax.rsqrt(meansq + 1e-06) * gain_ref[...][None, :]).astype(BF16)
    exchanges = [head_exchange(m, proj, got, x_send, x_recv) for m in range(3)]
    unit = jnp.where(
        lax.broadcasted_iota(jnp.int32, (D, D), 0) == lax.broadcasted_iota(jnp.int32, (D, D), 1),
        1.0,
        0.0,
    ).astype(BF16)

    def project(m):
        loads[m].wait()
        wt_scr[...] = nt(unit, w_scr[m]).astype(BF16)
        done = nt(wt_scr[...], normed).astype(BF16)
        for h in range(HEADS):
            proj[m, h] = done[h * HDIM : (h + 1) * HDIM]

    tall = SLAB // BLOCK

    def picker(c, carry):
        every = lax.broadcasted_iota(jnp.int32, (SLAB, CHUNK), 0)
        order = order_scr[:, pl.ds(pl.multiple_of(c * CHUNK, CHUNK), CHUNK)]
        pick = jnp.where(every == order, 1.0, 0.0).astype(BF16)
        pick_scr[pl.ds(c * tall, tall)] = pick.reshape(tall, BLOCK, CHUNK)
        return carry

    def move(m, first, last):
        def step(c, carry):
            rows = jnp.concatenate([got[m, b] for b in range(HEADS)], axis=1)
            pick = pick_scr[pl.ds(c * tall, tall)].reshape(SLAB, CHUNK)
            moved = nn(rows, pick).astype(BF16)
            for i in range(CHUNK // BLOCK):
                own[m, c * (CHUNK // BLOCK) + i] = moved[:, i * BLOCK : (i + 1) * BLOCK]
            return carry

        lax.fori_loop(first, last, step, 0)

    tables = (kt, vt, qt)
    rings = [
        ring_copies(
            m,
            own.at[m],
            tables[m],
            q_pos if m == QUERIES else kv_pos,
            on_q_ring if m == QUERIES else on_kv_ring,
            ring_send,
            ring_recv,
        )
        for m in range(3)
    ]

    def reorder_and_send(m, between=None):
        move(m, 0, CHUNKS // 2)
        rings[m](1).start()
        if between is not None:
            between()
        move(m, CHUNKS // 2, CHUNKS)
        rings[m](3).start()
        rings[m](0).start()
        rings[m](2).start()

    def pass_on(m, k):
        rings[m](k).wait_recv()
        rings[m](4 if k == 1 else 5).start()

    def received(m):
        for k in (0, 2, 4, 5):
            rings[m](k).wait_recv()

    def keep(m):
        got[m, head] = proj[m, head]

    def begin(m):
        exchanges[m][0]()

    def finish_near(m):
        exchanges[m][1]()

    def finish(m):
        exchanges[m][2]()

    project(KEYS)
    pl.semaphore_wait(barrier, len(partners))
    begin(KEYS)
    project(QUERIES)
    project(VALUES)
    order_scr[...] = order_ref[...][None, :]
    lax.fori_loop(0, CHUNKS, picker, 0)
    for m in range(3):
        keep(m)
    finish_near(KEYS)
    begin(QUERIES)
    finish(KEYS)
    reorder_and_send(KEYS)
    finish_near(QUERIES)
    begin(VALUES)
    finish(QUERIES)
    pass_on(KEYS, 1)
    reorder_and_send(QUERIES, lambda: pass_on(KEYS, 3))
    finish_near(VALUES)
    finish(VALUES)
    reorder_and_send(VALUES, lambda: pass_on(QUERIES, 1))
    pass_on(QUERIES, 3)
    for m in range(3):
        pos = q_pos if m == QUERIES else kv_pos
        tables[m][pl.ds(pos * CL, CL)] = own[m]

    def near(g):
        group = range(NEAR_GROUP)
        at = [g * NEAR_GROUP + u for u in group]
        cols = [[tiles_ref[t, q_pos * CL + c] for t in range(LOC)] for c in at]

        def joint(m):
            return lambda u, p: jnp.concatenate(
                [own[m, cols[u][2 * p]], own[m, cols[u][2 * p + 1]]], axis=1
            )

        queries = [turned(own[QUERIES, c]) for c in at]
        tops, ends = scores(
            queries, joint(KEYS), NEAR_PAIRS, s_scr, last=lambda u: own[KEYS, cols[u][LOC - 1]]
        )
        totals = [
            tall_sums(own[VALUES, cols[u][LOC - 1]], exponent(ends[u], tops[u])) for u in group
        ]
        for p in range(NEAR_PAIRS):
            for u in group:
                expo = exponent(s_scr[u * NEAR_PAIRS + p], tops[u])
                totals[u] += tall_sums(joint(VALUES)(u, p), expo)
        for u in group:
            near_scr[at[u]] = with_stats(totals[u], across(tops[u]))


    def far_tiles(at):
        cols = [[tiles_ref[LOC + t, c] for t in range(FAR)] for c in at]
        return cols, [[jnp.maximum(t, 0) for t in one] for one in cols]

    def joint_far(table, safe):
        return lambda u, p: jnp.concatenate(
            [table[safe[u][2 * p]], table[safe[u][2 * p + 1]]], axis=1
        )

    def far_scores(at):
        cols, safe = far_tiles(at)
        bias = [[jnp.where(t >= 0, 0.0, NEG) for t in one] for one in cols]
        return scores(
            [turned(qt[c]) for c in at],
            joint_far(kt, safe),
            FAR_PAIRS,
            s_scr,
            biases=[[(one[2 * p], one[2 * p + 1]) for p in range(FAR_PAIRS)] for one in bias],
        )[0]

    def far_rows(step, k):
        block = (q_pos + step) % RING
        return block, [block * CL + first_row(k) + u for u in range(PIECE)]

    def far_results(step, k):
        at = far_rows(step, k)[1] + far_rows(step, k + 1)[1]
        tops = far_scores(at)
        values = joint_far(vt, far_tiles(at)[1])
        totals = [None] * len(at)
        for p in range(FAR_PAIRS):
            for u in range(len(at)):
                expo = exponent(s_scr[u * FAR_PAIRS + p], tops[u])
                total = tall_sums(values(u, p), expo)
                totals[u] = total if p == 0 else totals[u] + total
        return [with_stats(total, across(top)) for total, top in zip(totals, tops)]

    def far_part(step, k):
        block = (q_pos + step) % RING
        for u, one in enumerate(far_results(step, k)):
            part[block, first_row(k + u // PIECE) + u % PIECE] = in_parts(one)


    def first_row(k):
        return (x + 3 - k) % RING * PIECE

    def rows(k):
        return pl.ds(first_row(k), PIECE)

    def back_copy(src, dst, k, step):
        return remote(src, dst, b_send.at[k], b_recv.at[k], on_q_ring(step))

    def direct(way, k):
        step = 1 + 2 * way
        src = part.at[(q_pos + step) % RING, rows(k)]
        return back_copy(src, back.at[way, rows(k)], 4 * way + k, step)

    def first_leg(k):
        return back_copy(
            part.at[(q_pos + 2) % RING, rows(k)], turn.at[k], 8 + k, 1 + 2 * (k % 2)
        )

    def second_leg(k):
        return back_copy(turn.at[k], back.at[2, rows(k)], 12 + k, 1 + 2 * (k % 2))

    def opposite(i, carry):
        far_part(2, 2 * i)
        first_leg(2 * i).start()
        first_leg(2 * i + 1).start()
        return carry

    def neighbours(i, carry):
        far_part(1, 2 * i)
        direct(0, 2 * i).start()
        direct(0, 2 * i + 1).start()
        for k in (2 * i, 2 * i + 1):
            first_leg(k).wait_recv()
            second_leg(k).start()
        far_part(3, 2 * i)
        direct(1, 2 * i).start()
        direct(1, 2 * i + 1).start()
        return carry

    def own_far(i, carry):
        for u, one in enumerate(far_results(0, 2 * i)):
            far_scr[i * 2 * PIECE + u] = one
        return carry

    def joined(c, i):
        values, tops, sums = [], [], []
        for tall_result in (near_scr[c], far_scr[i]):
            values.append(tall_result[:HDIM])
            sums.append(tall_result[HDIM : HDIM + 1])
            tops.append(tall_result[HDIM + TOP_HIGH : HDIM + TOP_HIGH + 1])
        for way in range(3):
            sent = back[way, c].astype(F32)
            values.append(sent[:HDIM])
            stat = [sent[HDIM + r : HDIM + r + 1] for r in range(STATS)]
            sums.append(stat[0] + stat[SUM_LOW])
            tops.append(stat[TOP_HIGH] + stat[TOP_MID] + stat[TOP_LOW])
        top = functools.reduce(jnp.maximum, tops)
        scales = [jnp.exp2((one - top) * SCALE2) for one in tops]
        whole = sum(a * b for a, b in zip(sums, scales))
        scales = [one / whole for one in scales]
        return sum(a * b for a, b in zip(values, scales)).astype(BF16)

    def out_copy(j, sender):
        return remote(
            stage.at[j], out_ref.at[sender], o_send.at[j], o_recv.at[sender], (line, j)
        )

    def close(k, carry):
        direct(0, k).wait_recv()
        direct(1, k).wait_recv()
        second_leg(k).wait_recv()
        for i in range(2):
            j = first_row(k) // 3 + i
            stage[j] = jnp.concatenate([joined(j * 3 + c, k * PIECE + i * 3 + c) for c in range(3)], axis=1)

            @pl.when(j != head)
            def _():
                out_copy(j, head).start()

            @pl.when(j == head)
            def _():
                out_ref[head] = stage[j]

        return carry

    def some_near(first, last):
        def one(g, carry):
            near(g)
            return carry

        lax.fori_loop(first, last, one, 0)

    some_near(0, 2)
    pass_on(VALUES, 1)
    some_near(2, 3)
    pass_on(VALUES, 3)
    some_near(3, CL // NEAR_GROUP)
    for m in range(3):
        received(m)
    lax.fori_loop(0, 2, opposite, 0)
    lax.fori_loop(0, 2, neighbours, 0)

    def own_and_close(i, carry):
        own_far(i, carry)
        return lax.fori_loop(2 * i, 2 * i + 2, close, carry)

    lax.fori_loop(0, 2, own_and_close, 0)

    for d in range(1, HEADS):
        out_copy((head + d) % HEADS, (head + d) % HEADS).wait_recv()
    for d in range(1, HEADS):
        out_copy((head + d) % HEADS, head).wait_send()
    for k in range(RING):
        direct(0, k).wait_send()
        direct(1, k).wait_send()
        first_leg(k).wait_send()
        second_leg(k).wait_send()
    for m in range(3):
        exchanges[m][3]()
        for k in range(6):
            rings[m](k).wait_send()


def layer(features, gain, order, tiles, wk, wv, wq):
    dma = pltpu.SemaphoreType.DMA
    return pl.pallas_call(
        layer_kernel,
        out_shape=pltpu.VMEM((HEADS, HDIM, ROWS), BF16),
        in_specs=[ANY, VMEM, VMEM, SMEM, ANY, ANY, ANY],
        out_specs=VMEM,
        scratch_shapes=[
            pltpu.VMEM((1, SLAB), jnp.int32),
            pltpu.VMEM((ROWS, D), BF16),
            pltpu.VMEM((3, D, D), BF16),
            pltpu.VMEM((D, D), BF16),
            pltpu.VMEM((3, HEADS, HDIM, ROWS), BF16),
            pltpu.VMEM((3, HEADS, HDIM, ROWS), BF16),
            pltpu.VMEM((CHUNKS * (SLAB // BLOCK), BLOCK, CHUNK), BF16),
            pltpu.VMEM((3, CL, HDIM, BLOCK), BF16),
            pltpu.VMEM((QROWS, HDIM, BLOCK), BF16),
            pltpu.VMEM((QROWS, HDIM, BLOCK), BF16),
            pltpu.VMEM((QROWS, HDIM, BLOCK), BF16),
            pltpu.VMEM((CL, TALL, BLOCK), F32),
            pltpu.VMEM((CL, TALL, BLOCK), F32),
            pltpu.VMEM((2 * PIECE * FAR_PAIRS, BLOCK, 2 * BLOCK), F32),
            pltpu.VMEM((RING, CL, TALL, BLOCK), BF16),
            pltpu.VMEM((3, CL, TALL, BLOCK), BF16),
            pltpu.VMEM((RING, PIECE, TALL, BLOCK), BF16),
            pltpu.VMEM((HEADS, HDIM, ROWS), BF16),
            dma((4,)),
            dma((3, HEADS)),
            dma((3, HEADS)),
            dma((3, 6)),
            dma((3, 6)),
            dma((4 * RING,)),
            dma((4 * RING,)),
            dma((HEADS,)),
            dma((HEADS,)),
        ],
        compiler_params=pltpu.CompilerParams(
            collective_id=1, has_side_effects=True, vmem_limit_bytes=LIMIT
        ),
    )(features, gain, order, tiles, wk, wv, wq)


def tile_positions(tile_cols):
    line, head, z, y, core = place()
    slabs = [
        (z * (1 - core) + p * core) * RING + p * (1 - core) + y * core for p in range(RING)
    ]
    cols = jnp.concatenate(
        [lax.dynamic_slice_in_dim(tile_cols.T, slab * CL, CL, 1) for slab in slabs], axis=1
    )
    slab, within = cols // CL, cols % CL
    slab_z, slab_y = slab // RING, slab % RING
    here = jnp.where(core == 0, slab_y == y, slab_z == z) & (cols >= 0)
    index = jnp.where(core == 0, slab_z, slab_y)
    is_near = lax.broadcasted_iota(jnp.int32, cols.shape, 0) < LOC
    return jnp.where(is_near, within, jnp.where(here, index * CL + within, -1))


def body(features, node_order, tile_cols, norm_gain, w_query, w_key, w_value, w_out):
    merged = layer(
        features,
        norm_gain,
        node_order,
        tile_positions(tile_cols),
        w_key,
        w_value,
        w_query,
    )
    return lax.dot_general(
        merged.reshape(D, ROWS), w_out, (((0,), (0,)), ((), ())), preferred_element_type=F32
    ).astype(BF16)


def solution(mesh):
    in_specs = (P(("loop", "head"), None), P("loop"), P(), P(), P(), P(), P(), P())
    out_specs = P(("loop", "head"), None)
    return jax.shard_map(body, mesh=mesh, in_specs=in_specs, out_specs=out_specs, check_vma=False)
```

```python
import functools
import math

import jax
import jax.numpy as jnp
from jax import lax
from jax.experimental import pallas as pl
from jax.experimental.pallas import tpu as pltpu
from jax.sharding import PartitionSpec as P

HEADS = 8
HDIM = 96
D = 768
BLOCK = 128
CL = 24
LOC = 21
FAR = 8
ROWS = 384
SLAB = 3072
RING = 4
QROWS = RING * CL
SCALE2 = math.log2(math.e) / math.sqrt(HDIM)
MESH = pl.DeviceIdType.MESH
VMEM = pl.BlockSpec(memory_space=pltpu.VMEM)
SMEM = pl.BlockSpec(memory_space=pltpu.SMEM)
ANY = pl.BlockSpec(memory_space=pl.ANY)
LIMIT = 54 * 1024 * 1024
NEG = -1e30
F32 = jnp.float32
BF16 = jnp.bfloat16
KEYS, VALUES, QUERIES = 0, 1, 2
HALF = CL // 2
CHUNK = 256
CHUNKS = SLAB // CHUNK
PIECE = 6
NEAR_GROUP = 4
NEAR_PAIRS = LOC // 2
FAR_PAIRS = FAR // 2
STATS = 16
TALL = HDIM + STATS
SUM_LOW, TOP_HIGH, TOP_MID, TOP_LOW = 4, 8, 11, 14


def nt(a, b):
    return lax.dot_general(a, b, (((1,), (1,)), ((), ())), preferred_element_type=F32)


def nn(a, b):
    return jnp.dot(a, b, preferred_element_type=F32)


def place():
    line = lax.axis_index("loop")
    head = lax.axis_index("head")
    z, y, core = line // RING, line % RING, head % 2
    return line, head, z, y, core


def on_kv_ring(step):
    line, head, z, y, core = place()
    return ((z + step * (1 - core)) % RING * RING + (y + step * core) % RING, head)


def on_q_ring(step):
    line, head, z, y, core = place()
    return ((z + step * core) % RING * RING + (y + step * (1 - core)) % RING, head)


def remote(src, dst, send, recv, device):
    return pltpu.make_async_remote_copy(
        src_ref=src,
        dst_ref=dst,
        send_sem=send,
        recv_sem=recv,
        device_id=device,
        device_id_type=MESH,
    )


def head_exchange(m, own, got, send, recv):
    line, head, z, y, core = place()
    x = head // 2
    own, got = own.at[m], got.at[m]
    near = [x * 2 + 1 - core]
    near += [(x + step) % RING * 2 + c for step in (1, 3) for c in range(2)]
    opposite = [(x + 2) % RING * 2 + c for c in range(2)]

    def to(k, target):
        return remote(
            own.at[target], got.at[head], send.at[m, k], recv.at[m, head], (line, target)
        )

    def arrived(source):
        remote(
            own.at[source], got.at[source], send.at[m, 0], recv.at[m, source], (line, source)
        ).wait_recv()

    def start():
        for k, target in enumerate(opposite + near):
            to(k, target).start()

    def finish_near():
        for source in near:
            arrived(source)

    def finish():
        for source in opposite:
            arrived(source)

    def drain():
        for k, target in enumerate(opposite + near):
            to(k, target).wait_send()

    return start, finish_near, finish, drain


def ring_copies(m, own, table, pos, device, send, recv):
    before, after = (pos + RING - 1) % RING, (pos + 1) % RING
    plan = [
        (None, HALF, 1),
        (None, 0, 1),
        (None, 0, RING - 1),
        (None, HALF, RING - 1),
        (before, 0, 1),
        (after, HALF, RING - 1),
    ]

    def copy(k):
        block, start, step = plan[k]
        if block is None:
            src = own.at[pl.ds(start, HALF)]
            block = pos
        else:
            src = table.at[pl.ds(block * CL + start, HALF)]
        dst = table.at[pl.ds(block * CL + start, HALF)]
        return remote(src, dst, send.at[m, k], recv.at[m, k], device(step))

    return copy


def scores(queries, keys_of, pairs, s_scr, last=None, biases=None):
    group = range(len(queries))
    tops = [None] * len(queries)
    for p in range(pairs):
        for u in group:
            score = nn(queries[u], keys_of(u, p))
            if biases is not None:
                low, high = biases[u][p]
                score = jnp.concatenate([score[:, :BLOCK] + low, score[:, BLOCK:] + high], axis=1)
            s_scr[u * pairs + p] = score
            tops[u] = score if p == 0 else jnp.maximum(tops[u], score)
    for u in group:
        tops[u] = jnp.maximum(tops[u][:, :BLOCK], tops[u][:, BLOCK:])
    ends = None
    if last is not None:
        ends = [nn(queries[u], last(u)) for u in group]
        for u in group:
            tops[u] = jnp.maximum(tops[u], ends[u])
    return [jnp.max(top, axis=1, keepdims=True) for top in tops], ends


def exponent(score, top):
    return jnp.exp2((score - top) * SCALE2).astype(BF16)


def tall_sums(values, expo):
    ones = jnp.ones((STATS, values.shape[1]), BF16)
    return nt(jnp.concatenate([values, ones], axis=0), expo)


def across(top):
    lane = lax.broadcasted_iota(jnp.int32, (BLOCK, BLOCK), 1)
    top = jnp.broadcast_to(top, (BLOCK, BLOCK))
    high = top.astype(BF16).astype(F32)
    rest = top - high
    mid = rest.astype(BF16).astype(F32)
    parts = jnp.where(lane == 0, high, jnp.where(lane == 1, mid, rest - mid))
    parts = jnp.where(lane < 3, parts, 0.0).astype(BF16)
    return nt(jnp.ones((STATS, BLOCK), BF16), parts)


def with_stats(total, top_rows):
    row = lax.broadcasted_iota(jnp.int32, (STATS, BLOCK), 0)
    stats = jnp.where(row < TOP_HIGH, total[HDIM:], top_rows)
    return jnp.concatenate([total[:HDIM], stats], axis=0)


def in_parts(tall):
    row = lax.broadcasted_iota(jnp.int32, (STATS, BLOCK), 0)
    is_mid = ((row >= SUM_LOW) & (row < TOP_HIGH)) | ((row >= TOP_MID) & (row < TOP_LOW))
    stats = tall[HDIM:]
    high = stats.astype(BF16).astype(F32)
    rest = stats - high
    mid = rest.astype(BF16).astype(F32)
    stats = jnp.where(is_mid, mid, jnp.where(row >= TOP_LOW, rest - mid, high))
    return jnp.concatenate([tall[:HDIM].astype(BF16), stats.astype(BF16)], axis=0)


def turned(block):
    return jnp.transpose(block.astype(F32)).astype(BF16)


def layer_kernel(
    feat_ref,
    gain_ref,
    order_ref,
    tiles_ref,
    wk_ref,
    wv_ref,
    wq_ref,
    out_ref,
    order_scr,
    feat_scr,
    w_scr,
    wt_scr,
    proj,
    got,
    pick_scr,
    own,
    kt,
    vt,
    qt,
    near_scr,
    far_scr,
    s_scr,
    part,
    back,
    turn,
    stage,
    w_sem,
    x_send,
    x_recv,
    ring_send,
    ring_recv,
    b_send,
    b_recv,
    o_send,
    o_recv,
):
    line, head, z, y, core = place()
    x = head // 2
    kv_pos = z * (1 - core) + y * core
    q_pos = z * core + y * (1 - core)
    feat_load = pltpu.make_async_copy(feat_ref, feat_scr, w_sem.at[3])
    feat_load.start()
    loads = [
        pltpu.make_async_copy(ref, w_scr.at[m], w_sem.at[m])
        for m, ref in enumerate((wk_ref, wv_ref, wq_ref))
    ]
    for m in (KEYS, QUERIES, VALUES):
        loads[m].start()
    partners = [on_kv_ring(1), on_kv_ring(3), on_q_ring(1), on_q_ring(3)]
    partners += [(line, (head + d) % HEADS) for d in range(1, HEADS)]
    barrier = pltpu.get_barrier_semaphore()
    for partner in partners:
        pl.semaphore_signal(barrier, inc=1, device_id=partner, device_id_type=MESH)

    feat_load.wait()
    wide = feat_scr[...].astype(F32)
    meansq = jnp.mean(wide * wide, axis=-1, keepdims=True)
    normed = (wide * lax.rsqrt(meansq + 1e-06) * gain_ref[...][None, :]).astype(BF16)
    exchanges = [head_exchange(m, proj, got, x_send, x_recv) for m in range(3)]
    unit = jnp.where(
        lax.broadcasted_iota(jnp.int32, (D, D), 0) == lax.broadcasted_iota(jnp.int32, (D, D), 1),
        1.0,
        0.0,
    ).astype(BF16)

    def project(m):
        loads[m].wait()
        wt_scr[...] = nt(unit, w_scr[m]).astype(BF16)
        done = nt(wt_scr[...], normed).astype(BF16)
        for h in range(HEADS):
            proj[m, h] = done[h * HDIM : (h + 1) * HDIM]

    tall = SLAB // BLOCK

    def picker(c, carry):
        every = lax.broadcasted_iota(jnp.int32, (SLAB, CHUNK), 0)
        order = order_scr[:, pl.ds(pl.multiple_of(c * CHUNK, CHUNK), CHUNK)]
        pick = jnp.where(every == order, 1.0, 0.0).astype(BF16)
        pick_scr[pl.ds(c * tall, tall)] = pick.reshape(tall, BLOCK, CHUNK)
        return carry

    def move(m, first, last):
        def step(c, carry):
            rows = jnp.concatenate([got[m, b] for b in range(HEADS)], axis=1)
            pick = pick_scr[pl.ds(c * tall, tall)].reshape(SLAB, CHUNK)
            moved = nn(rows, pick).astype(BF16)
            for i in range(CHUNK // BLOCK):
                own[m, c * (CHUNK // BLOCK) + i] = moved[:, i * BLOCK : (i + 1) * BLOCK]
            return carry

        lax.fori_loop(first, last, step, 0)

    tables = (kt, vt, qt)
    rings = [
        ring_copies(
            m,
            own.at[m],
            tables[m],
            q_pos if m == QUERIES else kv_pos,
            on_q_ring if m == QUERIES else on_kv_ring,
            ring_send,
            ring_recv,
        )
        for m in range(3)
    ]

    def reorder_and_send(m, between=None):
        move(m, 0, CHUNKS // 2)
        rings[m](1).start()
        if between is not None:
            between()
        move(m, CHUNKS // 2, CHUNKS)
        rings[m](3).start()
        rings[m](0).start()
        rings[m](2).start()

    def pass_on(m, k):
        rings[m](k).wait_recv()
        rings[m](4 if k == 1 else 5).start()

    def received(m):
        for k in (0, 2, 4, 5):
            rings[m](k).wait_recv()

    def keep(m):
        got[m, head] = proj[m, head]

    def begin(m):
        exchanges[m][0]()

    def finish_near(m):
        exchanges[m][1]()

    def finish(m):
        exchanges[m][2]()

    project(KEYS)
    pl.semaphore_wait(barrier, len(partners))
    begin(KEYS)
    project(QUERIES)
    project(VALUES)
    order_scr[...] = order_ref[...][None, :]
    lax.fori_loop(0, CHUNKS, picker, 0)
    for m in range(3):
        keep(m)
    finish_near(KEYS)
    begin(QUERIES)
    finish(KEYS)
    reorder_and_send(KEYS)
    finish_near(QUERIES)
    begin(VALUES)
    finish(QUERIES)
    pass_on(KEYS, 1)
    reorder_and_send(QUERIES, lambda: pass_on(KEYS, 3))
    finish_near(VALUES)
    finish(VALUES)
    reorder_and_send(VALUES, lambda: pass_on(QUERIES, 1))
    pass_on(QUERIES, 3)
    for m in range(3):
        pos = q_pos if m == QUERIES else kv_pos
        tables[m][pl.ds(pos * CL, CL)] = own[m]

    def near(g):
        group = range(NEAR_GROUP)
        at = [g * NEAR_GROUP + u for u in group]
        cols = [[tiles_ref[t, q_pos * CL + c] for t in range(LOC)] for c in at]

        def joint(m):
            return lambda u, p: jnp.concatenate(
                [own[m, cols[u][2 * p]], own[m, cols[u][2 * p + 1]]], axis=1
            )

        queries = [turned(own[QUERIES, c]) for c in at]
        tops, ends = scores(
            queries, joint(KEYS), NEAR_PAIRS, s_scr, last=lambda u: own[KEYS, cols[u][LOC - 1]]
        )
        totals = [
            tall_sums(own[VALUES, cols[u][LOC - 1]], exponent(ends[u], tops[u])) for u in group
        ]
        for p in range(NEAR_PAIRS):
            for u in group:
                expo = exponent(s_scr[u * NEAR_PAIRS + p], tops[u])
                totals[u] += tall_sums(joint(VALUES)(u, p), expo)
        for u in group:
            near_scr[at[u]] = with_stats(totals[u], across(tops[u]))


    def far_tiles(at):
        cols = [[tiles_ref[LOC + t, c] for t in range(FAR)] for c in at]
        return cols, [[jnp.maximum(t, 0) for t in one] for one in cols]

    def joint_far(table, safe):
        return lambda u, p: jnp.concatenate(
            [table[safe[u][2 * p]], table[safe[u][2 * p + 1]]], axis=1
        )

    def far_scores(at):
        cols, safe = far_tiles(at)
        bias = [[jnp.where(t >= 0, 0.0, NEG) for t in one] for one in cols]
        return scores(
            [turned(qt[c]) for c in at],
            joint_far(kt, safe),
            FAR_PAIRS,
            s_scr,
            biases=[[(one[2 * p], one[2 * p + 1]) for p in range(FAR_PAIRS)] for one in bias],
        )[0]

    def far_rows(step, k):
        block = (q_pos + step) % RING
        return block, [block * CL + first_row(k) + u for u in range(PIECE)]

    def far_results(step, k):
        at = far_rows(step, k)[1] + far_rows(step, k + 1)[1]
        tops = far_scores(at)
        values = joint_far(vt, far_tiles(at)[1])
        totals = [None] * len(at)
        for p in range(FAR_PAIRS):
            for u in range(len(at)):
                expo = exponent(s_scr[u * FAR_PAIRS + p], tops[u])
                total = tall_sums(values(u, p), expo)
                totals[u] = total if p == 0 else totals[u] + total
        return [with_stats(total, across(top)) for total, top in zip(totals, tops)]

    def far_part(step, k):
        block = (q_pos + step) % RING
        for u, one in enumerate(far_results(step, k)):
            part[block, first_row(k + u // PIECE) + u % PIECE] = in_parts(one)


    def first_row(k):
        return (x + 3 - k) % RING * PIECE

    def rows(k):
        return pl.ds(first_row(k), PIECE)

    def back_copy(src, dst, k, step):
        return remote(src, dst, b_send.at[k], b_recv.at[k], on_q_ring(step))

    def direct(way, k):
        step = 1 + 2 * way
        src = part.at[(q_pos + step) % RING, rows(k)]
        return back_copy(src, back.at[way, rows(k)], 4 * way + k, step)

    def first_leg(k):
        return back_copy(
            part.at[(q_pos + 2) % RING, rows(k)], turn.at[k], 8 + k, 1 + 2 * (k % 2)
        )

    def second_leg(k):
        return back_copy(turn.at[k], back.at[2, rows(k)], 12 + k, 1 + 2 * (k % 2))

    def opposite(i, carry):
        far_part(2, 2 * i)
        first_leg(2 * i).start()
        first_leg(2 * i + 1).start()
        return carry

    def pass_back(first):
        for k in (first, first + 1):
            first_leg(k).wait_recv()
            second_leg(k).start()

    def neighbours(i, carry):
        far_part(1, 2 * i)
        direct(0, 2 * i).start()
        direct(0, 2 * i + 1).start()

        @pl.when(i == 0)
        def _():
            pass_back(0)

        far_part(3, 2 * i)
        direct(1, 2 * i).start()
        direct(1, 2 * i + 1).start()

        @pl.when(i == 0)
        def _():
            pass_back(2)

        return carry

    def own_far(i, carry):
        for u, one in enumerate(far_results(0, 2 * i)):
            far_scr[i * 2 * PIECE + u] = one
        return carry

    def joined(c, i):
        values, tops, sums = [], [], []
        for tall_result in (near_scr[c], far_scr[i]):
            values.append(tall_result[:HDIM])
            sums.append(tall_result[HDIM : HDIM + 1])
            tops.append(tall_result[HDIM + TOP_HIGH : HDIM + TOP_HIGH + 1])
        for way in range(3):
            sent = back[way, c].astype(F32)
            values.append(sent[:HDIM])
            stat = [sent[HDIM + r : HDIM + r + 1] for r in range(STATS)]
            sums.append(stat[0] + stat[SUM_LOW])
            tops.append(stat[TOP_HIGH] + stat[TOP_MID] + stat[TOP_LOW])
        top = functools.reduce(jnp.maximum, tops)
        scales = [jnp.exp2((one - top) * SCALE2) for one in tops]
        whole = sum(a * b for a, b in zip(sums, scales))
        scales = [one / whole for one in scales]
        return sum(a * b for a, b in zip(values, scales)).astype(BF16)

    def out_copy(j, sender):
        return remote(
            stage.at[j], out_ref.at[sender], o_send.at[j], o_recv.at[sender], (line, j)
        )

    def close(k, carry):
        direct(0, k).wait_recv()
        direct(1, k).wait_recv()
        second_leg(k).wait_recv()
        for i in range(2):
            j = first_row(k) // 3 + i
            stage[j] = jnp.concatenate([joined(j * 3 + c, k * PIECE + i * 3 + c) for c in range(3)], axis=1)

            @pl.when(j != head)
            def _():
                out_copy(j, head).start()

            @pl.when(j == head)
            def _():
                out_ref[head] = stage[j]

        return carry

    def some_near(first, last):
        def one(g, carry):
            near(g)
            return carry

        lax.fori_loop(first, last, one, 0)

    some_near(0, 2)
    pass_on(VALUES, 1)
    some_near(2, 3)
    pass_on(VALUES, 3)
    some_near(3, CL // NEAR_GROUP)
    for m in range(3):
        received(m)
    lax.fori_loop(0, 2, opposite, 0)
    lax.fori_loop(0, 2, neighbours, 0)

    def own_and_close(i, carry):
        own_far(i, carry)
        return lax.fori_loop(2 * i, 2 * i + 2, close, carry)

    lax.fori_loop(0, 2, own_and_close, 0)

    for d in range(1, HEADS):
        out_copy((head + d) % HEADS, (head + d) % HEADS).wait_recv()
    for d in range(1, HEADS):
        out_copy((head + d) % HEADS, head).wait_send()
    for k in range(RING):
        direct(0, k).wait_send()
        direct(1, k).wait_send()
        first_leg(k).wait_send()
        second_leg(k).wait_send()
    for m in range(3):
        exchanges[m][3]()
        for k in range(6):
            rings[m](k).wait_send()


def layer(features, gain, order, tiles, wk, wv, wq):
    dma = pltpu.SemaphoreType.DMA
    return pl.pallas_call(
        layer_kernel,
        out_shape=pltpu.VMEM((HEADS, HDIM, ROWS), BF16),
        in_specs=[ANY, VMEM, VMEM, SMEM, ANY, ANY, ANY],
        out_specs=VMEM,
        scratch_shapes=[
            pltpu.VMEM((1, SLAB), jnp.int32),
            pltpu.VMEM((ROWS, D), BF16),
            pltpu.VMEM((3, D, D), BF16),
            pltpu.VMEM((D, D), BF16),
            pltpu.VMEM((3, HEADS, HDIM, ROWS), BF16),
            pltpu.VMEM((3, HEADS, HDIM, ROWS), BF16),
            pltpu.VMEM((CHUNKS * (SLAB // BLOCK), BLOCK, CHUNK), BF16),
            pltpu.VMEM((3, CL, HDIM, BLOCK), BF16),
            pltpu.VMEM((QROWS, HDIM, BLOCK), BF16),
            pltpu.VMEM((QROWS, HDIM, BLOCK), BF16),
            pltpu.VMEM((QROWS, HDIM, BLOCK), BF16),
            pltpu.VMEM((CL, TALL, BLOCK), F32),
            pltpu.VMEM((CL, TALL, BLOCK), F32),
            pltpu.VMEM((2 * PIECE * FAR_PAIRS, BLOCK, 2 * BLOCK), F32),
            pltpu.VMEM((RING, CL, TALL, BLOCK), BF16),
            pltpu.VMEM((3, CL, TALL, BLOCK), BF16),
            pltpu.VMEM((RING, PIECE, TALL, BLOCK), BF16),
            pltpu.VMEM((HEADS, HDIM, ROWS), BF16),
            dma((4,)),
            dma((3, HEADS)),
            dma((3, HEADS)),
            dma((3, 6)),
            dma((3, 6)),
            dma((4 * RING,)),
            dma((4 * RING,)),
            dma((HEADS,)),
            dma((HEADS,)),
        ],
        compiler_params=pltpu.CompilerParams(
            collective_id=1, has_side_effects=True, vmem_limit_bytes=LIMIT
        ),
    )(features, gain, order, tiles, wk, wv, wq)


def tile_positions(tile_cols):
    line, head, z, y, core = place()
    slabs = [
        (z * (1 - core) + p * core) * RING + p * (1 - core) + y * core for p in range(RING)
    ]
    cols = jnp.concatenate(
        [lax.dynamic_slice_in_dim(tile_cols.T, slab * CL, CL, 1) for slab in slabs], axis=1
    )
    slab, within = cols // CL, cols % CL
    slab_z, slab_y = slab // RING, slab % RING
    here = jnp.where(core == 0, slab_y == y, slab_z == z) & (cols >= 0)
    index = jnp.where(core == 0, slab_z, slab_y)
    is_near = lax.broadcasted_iota(jnp.int32, cols.shape, 0) < LOC
    return jnp.where(is_near, within, jnp.where(here, index * CL + within, -1))


def body(features, node_order, tile_cols, norm_gain, w_query, w_key, w_value, w_out):
    merged = layer(
        features,
        norm_gain,
        node_order,
        tile_positions(tile_cols),
        w_key,
        w_value,
        w_query,
    )
    return lax.dot_general(
        merged.reshape(D, ROWS), w_out, (((0,), (0,)), ((), ())), preferred_element_type=F32
    ).astype(BF16)


def solution(mesh):
    in_specs = (P(("loop", "head"), None), P("loop"), P(), P(), P(), P(), P(), P())
    out_specs = P(("loop", "head"), None)
    return jax.shard_map(body, mesh=mesh, in_specs=in_specs, out_specs=out_specs, check_vma=False)
```
